32 devices in a mesh: snode: 8 (over z, x), rhs: 4 (over y, core).
Axes of the slice: x: 2, y: 2, z: 4, core: 2. Of those that a mesh axis runs over, the one named last changes fastest.
Arguments:
- right_sides: float32 [3, 16, 256, 512], P(None, 'snode', None, 'rhs'), may hold values from -6 to 6
- diag_inverse: float32 [3, 16, 256, 256], P(None, 'snode', 'rhs')
- off_diagonal: bfloat16 [2, 16, 1024, 256], P(None, 'snode'), may hold values from -0.125 to 0.125
- target_snode: int32 [2, 16, 64], P(None, 'snode'), may hold values from 0 to 15, as said below
- target_block: int32 [2, 16, 64], P(None, 'snode'), may hold values from 0 to 15
Outputs:
- solution: float32 [3, 16, 256, 512], P(None, 'snode', None, 'rhs')
The draws below stay inside these ranges and needn't reach their ends.
Inputs may be any that keep to these rules, and one draw needn't show every extreme that they name: `target_snode`: each entry is a supernode's position in the next level; the supernodes at positions i * 2 to i * 2 + 1 belong to index i of snode. Of one level's blocks held by one index of snode, at most 32 name supernodes of any one index, and some index receives exactly 32 from every index in every level.
All inputs are finite; a program needn't handle non-finite values.
Results may differ from the reference program's by a relative error of at most 0.0038.
Values may be sent and summed in bfloat16 or wider, within the bound.
A program may use at most 64 MiB of HBM per device.

```python
import jax
import jax.numpy as jnp
from jax import lax

W = 256
K = 64
BR = 16
LEVELS = 3
SPL = 2
RHS = 512
NSN = 16
CAP = 32
HOT = 1


def draw_diag_inverse(key, part):
    shape = (LEVELS, NSN, W, W)
    diag_key, noise_key = jax.random.split(key)
    identity = jnp.eye(W, dtype=jnp.float32)
    scales = jnp.exp(jax.random.uniform(diag_key, (LEVELS, NSN, W, 1), jnp.float32, -0.7, 0.4))
    noise = jax.random.normal(noise_key, shape, jnp.float32) * (0.4 / W ** 0.5)
    return identity * scales + noise


def route_level(key):
    owners_count = NSN // SPL
    outgoing = SPL * K
    hot_key, device_key = jax.random.split(key)
    shuffled = jax.random.permutation(hot_key, owners_count).astype(jnp.int32)
    hot_slots = jnp.repeat(shuffled[:HOT], CAP)
    cold_slots = jnp.repeat(shuffled[HOT:], CAP)

    def one_sender(sender):
        pick_key, mix_key, place_key = jax.random.split(jax.random.fold_in(device_key, sender), 3)
        picked = cold_slots[jax.random.permutation(pick_key, cold_slots.shape[0])[:outgoing - HOT * CAP]]
        owners = jnp.concatenate([hot_slots, picked])
        owners = owners[jax.random.permutation(mix_key, outgoing)]
        position = jax.random.randint(place_key, (outgoing,), 0, SPL, jnp.int32)
        return (owners * SPL + position).reshape(SPL, K)
    senders = jnp.arange(owners_count, dtype=jnp.int32)
    return jax.vmap(one_sender)(senders).reshape(NSN, K)


def draw_target_snode(key, part):
    tiers = [route_level(jax.random.fold_in(key, 11 + height)) for height in range(LEVELS - 1)]
    return jnp.stack(tiers, axis=0).astype(jnp.int32)


def place_ends(drawn, key, low, top_value):
    shape = drawn.shape
    place = [jax.random.randint(jax.random.fold_in(key, axis), (), 0, shape[axis]) for axis in range(len(shape))]
    drawn = drawn.at[tuple(place)].set(low)
    longest = shape.index(max(shape))
    place[longest] = (place[longest] + 1) % shape[longest]
    return drawn.at[tuple(place)].set(top_value)


def shard_levels(rng, extent, shards, smallest, high):
    def one(dim, shards_of):
        draws = jax.random.uniform(jax.random.fold_in(jax.random.fold_in(rng, 6), dim), (shards_of,), jnp.float32, smallest / len(shards), high / len(shards))
        return jnp.repeat(jnp.exp(draws), extent[dim] // shards_of).reshape((-1,) + (1,) * (len(extent) - dim - 1))

    factor_of = one(*shards[0])
    for cut in shards[1:]:
        factor_of = factor_of * one(*cut)
    return factor_of


def normal_values(rng, extent, spread, limit, pieces=(), kind=jnp.bfloat16):
    level = shard_levels(rng, extent, pieces, -0.22, 0.18) if pieces else 1.0
    values = jax.random.normal(rng, extent, jnp.float32) * spread * level
    return jnp.minimum(jnp.maximum(values, -limit), limit).astype(kind)


def setup_inputs(seed: int = 0) -> dict:
    keys = jax.random.split(jax.random.key(seed), 6)
    return {
        "right_sides": normal_values(keys[0], (LEVELS, NSN, W, RHS), 1.0, 6.0, ((1, 8), (3, 4)), jnp.float32),
        "diag_inverse": draw_diag_inverse(jax.random.fold_in(keys[5], 71), 0),
        "off_diagonal": normal_values(keys[2], (LEVELS - 1, NSN, K * BR, W), (2 * K * BR) ** -0.5, 0.125, ((1, 8),)),
        "target_snode": draw_target_snode(jax.random.fold_in(keys[5], 71), 0),
        "target_block": place_ends(jax.random.randint(keys[4], (LEVELS - 1, NSN, K), 0, W // BR), jax.random.fold_in(keys[4], 1), 0, (W // BR) - 1).astype(jnp.int32),
    }


def reference(right_sides, diag_inverse, off_diagonal, target_snode, target_block):
    precise = lax.Precision.HIGHEST
    row_blocks = W // BR
    columns = right_sides.shape[3]
    solved = []
    residual = right_sides[0]
    for height in range(LEVELS):
        forward = jnp.einsum("svw,swr->svr", diag_inverse[height], residual, precision=precise)
        solved.append(forward)
        if height + 1 < LEVELS:
            rounded = lax.optimization_barrier(forward.astype(jnp.bfloat16)).astype(jnp.float32)
            update = jnp.einsum("skw,swr->skr", off_diagonal[height].astype(jnp.float32), rounded)
            update = lax.optimization_barrier(update.astype(jnp.bfloat16)).astype(jnp.float32)
            update = update.reshape(NSN * K, BR, columns)
            row_index = (target_snode[height] * row_blocks + target_block[height]).reshape(NSN * K).astype(jnp.int32)
            accumulated = jnp.zeros((NSN * row_blocks, BR, columns), jnp.float32).at[row_index].add(update)
            residual = right_sides[height + 1] - accumulated.reshape(NSN, W, columns)
    answer = [None] * LEVELS
    answer[LEVELS - 1] = jnp.einsum("swv,swr->svr", diag_inverse[LEVELS - 1], solved[LEVELS - 1], precision=precise)
    for height in range(LEVELS - 2, -1, -1):
        above_rows = lax.optimization_barrier(answer[height + 1].astype(jnp.bfloat16)).astype(jnp.float32)
        above_rows = above_rows.reshape(NSN * row_blocks, BR, columns)
        row_index = (target_snode[height] * row_blocks + target_block[height]).reshape(NSN * K).astype(jnp.int32)
        block_rows = above_rows[row_index].reshape(NSN, K * BR, columns)
        carried = solved[height] - jnp.einsum("skw,skr->swr", off_diagonal[height].astype(jnp.float32), block_rows)
        answer[height] = jnp.einsum("swv,swr->svr", diag_inverse[height], carried, precision=precise)
    return jnp.stack(answer, axis=0)
```

```python
import functools

import jax
import jax.numpy as jnp
from jax import lax
from jax.experimental import pallas as pl
from jax.experimental.pallas import tpu as pltpu
from jax.sharding import PartitionSpec as P

BR = 16


def on_device(right_sides, diag_inverse, off_diagonal, target_snode, target_block):
    precise = lax.Precision.HIGHEST
    levels = right_sides.shape[0]
    local_nodes = right_sides.shape[1]
    order_size = right_sides.shape[2]
    columns = right_sides.shape[3]
    per_node = target_snode.shape[2]
    row_blocks = order_size // BR
    devices = lax.axis_size("snode")
    outgoing = local_nodes * per_node
    capacity = 2 * outgoing // devices
    slot_count = devices * capacity
    local_rows = local_nodes * row_blocks
    front_count = 1
    front_width = columns // front_count
    full_diag = [
        lax.all_gather(diag_inverse[height], "rhs", axis=1, tiled=True) for height in range(levels)
    ]
    block_order = lax.iota(jnp.int32, outgoing)
    slot_ids = lax.iota(jnp.int32, slot_count)
    row_ids = lax.iota(jnp.int32, local_rows)
    routes = []
    for height in range(levels - 1):
        flat_target = target_snode[height].reshape(outgoing)
        owner_dev = flat_target // local_nodes
        target_code = flat_target % local_nodes * row_blocks + target_block[height].reshape(
            outgoing
        )
        earlier = (owner_dev[:, None] == owner_dev[None, :]) & (
            block_order[None, :] < block_order[:, None]
        )
        destination = owner_dev * capacity + jnp.sum(earlier.astype(jnp.int32), axis=1)
        placed = destination[None, :] == slot_ids[:, None]
        source = jnp.max(jnp.where(placed, block_order[None, :], -1), axis=1)
        slot_code = jnp.max(jnp.where(placed, target_code[None, :], -1), axis=1).reshape(
            devices, capacity
        )
        routes.append((destination, source, slot_code))
    residual_list = [right_sides[0]]
    lower_sols = [[]]
    arrivals = [[]]
    for height in range(levels):
        front = 0
        solve_result = jnp.einsum(
            "svw,swr->svr", full_diag[height], residual_list[front], precision=precise
        )
        lower_sols[front].append(solve_result)
        if height + 1 < levels:
            destination, source, slot_code = routes[height]
            update = jnp.einsum(
                "skw,swr->skr",
                off_diagonal[height],
                solve_result.astype(jnp.bfloat16),
                preferred_element_type=jnp.float32,
            )
            update = update.astype(jnp.bfloat16).reshape(outgoing, BR * front_width)
            outbound = jnp.where(
                (source >= 0)[:, None], update[jnp.maximum(source, 0)], jnp.zeros((), jnp.bfloat16)
            )
            outbound = outbound.reshape(devices, capacity, BR * front_width)
            inbound, inbound_code = (
                lax.all_to_all(outbound, "snode", split_axis=0, concat_axis=0, tiled=True),
                lax.all_to_all(slot_code, "snode", split_axis=0, concat_axis=0, tiled=True),
            )
            arrived = inbound_code.reshape(slot_count)
            arrivals[front].append(arrived)
            gather_table = (arrived[None, :] == row_ids[:, None]).astype(jnp.bfloat16)
            summed = jnp.dot(
                gather_table,
                inbound.reshape(slot_count, BR * front_width),
                preferred_element_type=jnp.float32,
            )
            summed = summed.reshape(local_nodes, order_size, front_width)
            upcoming = right_sides[height + 1]
            residual_list[front] = upcoming - summed
    answer = [[None] * levels]
    for height in range(levels - 1, -1, -1):
        front = 0
        if height == levels - 1:
            carried = lower_sols[front][height]
        else:
            destination, source, slot_code = routes[height]
            above_rows = (
                answer[front][height + 1].astype(jnp.bfloat16).reshape(local_rows, BR * front_width)
            )
            arrived = arrivals[front][height]
            outbound = jnp.where(
                (arrived >= 0)[:, None],
                above_rows[jnp.maximum(arrived, 0)],
                jnp.zeros((), jnp.bfloat16),
            )
            outbound = outbound.reshape(devices, capacity, BR * front_width)
            returned = lax.all_to_all(outbound, "snode", split_axis=0, concat_axis=0, tiled=True)
            block_rows = returned.reshape(slot_count, BR * front_width)[destination]
            block_rows = block_rows.reshape(local_nodes, per_node * BR, front_width)
            carried = lower_sols[front][height] - jnp.einsum(
                "skw,skr->swr", off_diagonal[height], block_rows, preferred_element_type=jnp.float32
            )
        result = jnp.einsum("swv,swr->svr", full_diag[height], carried, precision=precise)
        answer[front][height] = result
    stacked = [answer[0][height] for height in range(levels)]
    return jnp.stack(stacked, axis=0)


MESH = pl.DeviceIdType.MESH
PAIR = 2


def mm(a, b):
    return jnp.dot(a, b, preferred_element_type=jnp.float32)


def split(a):
    high = a.astype(jnp.bfloat16)
    return high, (a - high.astype(jnp.float32)).astype(jnp.bfloat16)


def mm3(a_high, a_low, b):
    cols = b.shape[1]
    b_high, b_low = split(b)
    wide = mm(a_high, jnp.concatenate([b_high, b_low], axis=1))
    return wide[:, :cols] + wide[:, cols:] + mm(a_low, b_high)


def dense_kernel(
    n, parts, rs_ref, dg_ref, od_ref, codev_ref, codes_ref, out_ref,
    full, diag_t, od_t, low, upd, nat, part, rx, ru, rd, zs, above, picked,
    dsend, drecv, xsend, xrecv, zsend, urecv, drecv2, asend, arecv, bsend, brecv,
):
    levels, local, order, cols = rs_ref.shape
    shard = dg_ref.shape[2]
    outgoing = codev_ref.shape[2]
    per_node = outgoing // local
    local_rows = local * order // BR
    line = n // PAIR
    ymany = parts // PAIR
    me = lax.axis_index("snode")
    z, x = me // PAIR, me % PAIR
    mine = lax.axis_index("rhs")
    yy, cc = mine // PAIR, mine % PAIR
    mate = {"snode": z * PAIR + (1 - x)}
    over = {"snode": (z + 1) * PAIR + x}
    under = {"snode": (z - 1) * PAIR + x}
    twin = {"rhs": yy * PAIR + (1 - cc)}
    sides = [(yy + k) % ymany for k in range(1, ymany)]

    def remote(src, dst, s_sem, r_sem, where):
        return pltpu.make_async_remote_copy(
            src_ref=src, dst_ref=dst, send_sem=s_sem, recv_sem=r_sem,
            device_id=where, device_id_type=MESH,
        )

    barrier = pltpu.get_barrier_semaphore()

    def greet(where):
        pl.semaphore_signal(barrier, inc=1, device_id=where, device_id_type=MESH)

    greet(mate)
    greet(twin)
    for side in sides:
        greet({"rhs": side * PAIR + cc})

    @pl.when(z > 0)
    def _():
        greet(under)

    @pl.when(z < line - 1)
    def _():
        greet(over)

    ends = jnp.where(z > 0, 1, 0) + jnp.where(z < line - 1, 1, 0)
    pl.semaphore_wait(barrier, 1 + ymany + ends)

    sent = []
    gather = []
    for h in range(levels):
        near = []
        for k, side in enumerate(sides):
            copy = remote(dg_ref.at[h], full.at[h, mine], dsend.at[h, k], drecv.at[h, k],
                          {"rhs": side * PAIR + cc})
            copy.start()
            near.append(copy)
        own = remote(dg_ref.at[h], full.at[h, mine], dsend.at[h, ymany], drecv.at[h, ymany], twin)
        own.start()
        gather.append((near, own))
    for h in range(levels):
        full[h, mine] = dg_ref[h]

    def finish_gather(h):
        near, own = gather[h]
        hops = []
        for k, copy in enumerate(near):
            copy.wait_recv()
            origin = ((yy + ymany - 1 - k) % ymany) * PAIR + cc
            hop = remote(full.at[h, origin], full.at[h, origin], dsend.at[h, ymany + 1 + k],
                         drecv.at[h, ymany + 1 + k], twin)
            hop.start()
            hops.append(hop)
        own.wait_recv()
        for hop in hops:
            hop.wait_recv()
        sent.extend(near + [own] + hops)

    def diag(h, s):
        return full[h, :, s].reshape(order, order)

    def forward(h, s, residual):
        high, low_part = split(diag(h, s))
        low[h, s] = mm3(high, low_part, residual)

    def backward(h, s, carried):
        out_ref[h, s] = mm3(diag_t[h, s, 0], diag_t[h, s, 1], carried)

    def prepare(h):
        for s in range(local):
            high, low_part = split(diag(h, s).T)
            diag_t[h, s, 0] = high
            diag_t[h, s, 1] = low_part

    finish_gather(0)
    for s in range(local):
        forward(0, s, rs_ref[0, s])

    for h in range(levels - 1):
        for s in range(local):
            upd[pl.ds(s * per_node * BR, per_node * BR), :] = mm(
                od_ref[h, s], low[h, s].astype(jnp.bfloat16)
            )
        rows = lax.broadcasted_iota(jnp.int32, (n * local_rows, outgoing), 0)
        table = jnp.where(rows == codev_ref[h], 1.0, 0.0).astype(jnp.bfloat16)
        for r in range(BR):
            piece = upd[pl.ds(r, outgoing, stride=BR), :].astype(jnp.bfloat16)
            summed = mm(table, piece).astype(jnp.bfloat16)
            for d in range(n):
                part[h, d, r * local_rows:(r + 1) * local_rows, :] = (
                    summed[d * local_rows:(d + 1) * local_rows]
                )

        for zz in range(line):
            @pl.when(z == zz)
            def _(zz=zz):
                for d in sorted(range(line), key=lambda d: -abs(d - zz)):
                    remote(part.at[h, d * PAIR + (1 - x)], rx.at[h, d], xsend.at[h, d],
                           xrecv.at[h, d], mate).start()

        if h == 0:
            for later in range(1, levels):
                finish_gather(later)
        prepare(h)
        if h == levels - 2:
            prepare(levels - 1)
        for s in range(local):
            od_t[h, s] = od_ref[h, s].T

        for zz in range(line):
            @pl.when(z == zz)
            def _(zz=zz):
                for d in sorted(range(line), key=lambda d: -abs(d - zz)):
                    remote(part.at[h, d * PAIR + (1 - x)], rx.at[h, d], xsend.at[h, d],
                           xrecv.at[h, d], mate).wait_recv()
                    total = part[h, d * PAIR + x].astype(jnp.float32) + rx[h, d].astype(jnp.float32)
                    if d >= zz and zz > 0:
                        remote(zs.at[h, d], ru.at[h, d], zsend.at[h, d], urecv.at[h, d],
                               under).wait_recv()
                        total = total + ru[h, d].astype(jnp.float32)
                    if d <= zz and zz < line - 1:
                        remote(zs.at[h, d], rd.at[h, d], zsend.at[h, d], drecv2.at[h, d],
                               over).wait_recv()
                        total = total + rd[h, d].astype(jnp.float32)
                    if d != zz:
                        zs[h, d] = total.astype(jnp.bfloat16)
                    if d > zz:
                        remote(zs.at[h, d], ru.at[h, d], zsend.at[h, d], urecv.at[h, d],
                               over).start()
                    elif d < zz:
                        remote(zs.at[h, d], rd.at[h, d], zsend.at[h, d], drecv2.at[h, d],
                               under).start()
                    else:
                        for r in range(BR):
                            nat[pl.ds(r, local_rows, stride=BR), :] = (
                                total[r * local_rows:(r + 1) * local_rows]
                            )
        for s in range(local):
            forward(h + 1, s, rs_ref[h + 1, s] - nat[pl.ds(s * order, order), :])

    for s in range(local):
        backward(levels - 1, s, low[levels - 1, s])

    for h in range(levels - 2, -1, -1):
        above[h][me] = out_ref[h + 1].reshape(local_rows, BR, cols).astype(jnp.bfloat16)

        def hop(s, where, sem_s, sem_r, col):
            slot = above[h].at[s * PAIR + col]
            return remote(slot, slot, sem_s, sem_r, where)

        for zz in range(line):
            @pl.when(z == zz)
            def _(zz=zz):
                for s in sorted(range(line), key=lambda s: abs(s - zz)):
                    if s != zz:
                        hop(s, mate, asend.at[h, 0, s], arecv.at[h, s], x).wait_recv()
                    if s <= zz and zz < line - 1:
                        hop(s, over, asend.at[h, 0, s], arecv.at[h, s], x).start()
                    if s >= zz and zz > 0:
                        hop(s, under, asend.at[h, 1, s], arecv.at[h, s], x).start()
                    hop(s, mate, bsend.at[h, s], brecv.at[h, s], x).start()
        for s in range(line):
            hop(s, mate, bsend.at[h, s], brecv.at[h, s], 1 - x).wait_recv()
        for k in range(outgoing):
            picked[pl.ds(k * BR, BR), :] = above[h][
                codes_ref[h, k] // local_rows, codes_ref[h, k] % local_rows
            ]
        for s in range(local):
            carried = low[h, s] - mm(
                od_t[h, s], picked[pl.ds(s * per_node * BR, per_node * BR), :]
            )
            backward(h, s, carried)

    for copy in sent:
        copy.wait_send()
    for h in range(levels - 1):
        for d in range(line):
            remote(part.at[h, d * PAIR + (1 - x)], rx.at[h, d], xsend.at[h, d],
                   xrecv.at[h, d], mate).wait_send()
            slot = above[h].at[d * PAIR + x]
            remote(slot, slot, bsend.at[h, d], brecv.at[h, d], mate).wait_send()
        for zz in range(line):
            @pl.when(z == zz)
            def _(zz=zz):
                for d in range(line):
                    slot = above[h].at[d * PAIR + x]
                    if d != zz:
                        remote(zs.at[h, d], ru.at[h, d], zsend.at[h, d], urecv.at[h, d],
                               mate).wait_send()
                    if d <= zz and zz < line - 1:
                        remote(slot, slot, asend.at[h, 0, d], arecv.at[h, d], mate).wait_send()
                    if d >= zz and zz > 0:
                        remote(slot, slot, asend.at[h, 1, d], arecv.at[h, d], mate).wait_send()


def dense_on_device(right_sides, diag_inverse, off_diagonal, target_snode, target_block):
    levels, local, order, cols = right_sides.shape
    n, parts = lax.axis_size("snode"), lax.axis_size("rhs")
    outgoing = local * target_snode.shape[2]
    row_blocks = order // BR
    local_rows = local * row_blocks
    chunk = local_rows * BR
    line = n // PAIR
    ymany = parts // PAIR
    code = (target_snode * row_blocks + target_block).reshape(levels - 1, outgoing)
    bf, f32 = jnp.bfloat16, jnp.float32
    steps = levels - 1
    dma = pltpu.SemaphoreType.DMA
    whole = pl.BlockSpec(memory_space=pltpu.VMEM)
    return pl.pallas_call(
        functools.partial(dense_kernel, n, parts),
        out_shape=jax.ShapeDtypeStruct(right_sides.shape, f32),
        in_specs=[whole] * 4 + [pl.BlockSpec(memory_space=pltpu.SMEM)],
        out_specs=whole,
        scratch_shapes=[
            pltpu.VMEM((levels, parts) + diag_inverse.shape[1:], f32),
            pltpu.VMEM((levels, local, 2, order, order), bf),
            pltpu.VMEM((steps, local, order, off_diagonal.shape[2]), bf),
            pltpu.VMEM(right_sides.shape, f32),
            pltpu.VMEM((outgoing * BR, cols), f32),
            pltpu.VMEM((chunk, cols), f32),
            pltpu.VMEM((steps, n, chunk, cols), bf),
            pltpu.VMEM((steps, line, chunk, cols), bf),
            pltpu.VMEM((steps, line, chunk, cols), bf),
            pltpu.VMEM((steps, line, chunk, cols), bf),
            pltpu.VMEM((steps, line, chunk, cols), bf),
            [pltpu.VMEM((n, local_rows, BR, cols), bf)] * steps,
            pltpu.VMEM((outgoing * BR, cols), bf),
            dma((levels, 2 * ymany)),
            dma((levels, 2 * ymany)),
            dma((steps, line)),
            dma((steps, line)),
            dma((steps, line)),
            dma((steps, line)),
            dma((steps, line)),
            dma((steps, 2, line)),
            dma((steps, line)),
            dma((steps, line)),
            dma((steps, line)),
        ],
        compiler_params=pltpu.CompilerParams(
            collective_id=0, has_side_effects=True, vmem_limit_bytes=48 * 1024 * 1024
        ),
    )(right_sides, diag_inverse, off_diagonal, code.reshape(steps, 1, outgoing), code)


def program(right_sides, diag_inverse, off_diagonal, target_snode, target_block):
    n, parts = lax.axis_size("snode"), lax.axis_size("rhs")
    capacity = 2 * right_sides.shape[1] * target_snode.shape[2] // n
    local_rows = right_sides.shape[1] * right_sides.shape[2] // BR
    dense = capacity >= local_rows and n % PAIR == 0 and parts % PAIR == 0
    body = dense_on_device if dense else on_device
    return body(right_sides, diag_inverse, off_diagonal, target_snode, target_block)


def solution(mesh):
    in_specs = (
        P(None, "snode", None, "rhs"),
        P(None, "snode", "rhs", None),
        P(None, "snode", None, None),
        P(None, "snode", None),
        P(None, "snode", None),
    )
    out_specs = P(None, "snode", None, "rhs")
    return jax.shard_map(
        program, mesh=mesh, in_specs=in_specs, out_specs=out_specs, check_vma=False
    )
```

```python
import functools

import jax
import jax.numpy as jnp
from jax import lax
from jax.experimental import pallas as pl
from jax.experimental.pallas import tpu as pltpu
from jax.sharding import PartitionSpec as P

BR = 16


def on_device(right_sides, diag_inverse, off_diagonal, target_snode, target_block):
    precise = lax.Precision.HIGHEST
    levels = right_sides.shape[0]
    local_nodes = right_sides.shape[1]
    order_size = right_sides.shape[2]
    columns = right_sides.shape[3]
    per_node = target_snode.shape[2]
    row_blocks = order_size // BR
    devices = lax.axis_size("snode")
    outgoing = local_nodes * per_node
    capacity = 2 * outgoing // devices
    slot_count = devices * capacity
    local_rows = local_nodes * row_blocks
    front_count = 1
    front_width = columns // front_count
    full_diag = [
        lax.all_gather(diag_inverse[height], "rhs", axis=1, tiled=True) for height in range(levels)
    ]
    block_order = lax.iota(jnp.int32, outgoing)
    slot_ids = lax.iota(jnp.int32, slot_count)
    row_ids = lax.iota(jnp.int32, local_rows)
    routes = []
    for height in range(levels - 1):
        flat_target = target_snode[height].reshape(outgoing)
        owner_dev = flat_target // local_nodes
        target_code = flat_target % local_nodes * row_blocks + target_block[height].reshape(
            outgoing
        )
        earlier = (owner_dev[:, None] == owner_dev[None, :]) & (
            block_order[None, :] < block_order[:, None]
        )
        destination = owner_dev * capacity + jnp.sum(earlier.astype(jnp.int32), axis=1)
        placed = destination[None, :] == slot_ids[:, None]
        source = jnp.max(jnp.where(placed, block_order[None, :], -1), axis=1)
        slot_code = jnp.max(jnp.where(placed, target_code[None, :], -1), axis=1).reshape(
            devices, capacity
        )
        routes.append((destination, source, slot_code))
    residual_list = [right_sides[0]]
    lower_sols = [[]]
    arrivals = [[]]
    for height in range(levels):
        front = 0
        solve_result = jnp.einsum(
            "svw,swr->svr", full_diag[height], residual_list[front], precision=precise
        )
        lower_sols[front].append(solve_result)
        if height + 1 < levels:
            destination, source, slot_code = routes[height]
            update = jnp.einsum(
                "skw,swr->skr",
                off_diagonal[height],
                solve_result.astype(jnp.bfloat16),
                preferred_element_type=jnp.float32,
            )
            update = update.astype(jnp.bfloat16).reshape(outgoing, BR * front_width)
            outbound = jnp.where(
                (source >= 0)[:, None], update[jnp.maximum(source, 0)], jnp.zeros((), jnp.bfloat16)
            )
            outbound = outbound.reshape(devices, capacity, BR * front_width)
            inbound, inbound_code = (
                lax.all_to_all(outbound, "snode", split_axis=0, concat_axis=0, tiled=True),
                lax.all_to_all(slot_code, "snode", split_axis=0, concat_axis=0, tiled=True),
            )
            arrived = inbound_code.reshape(slot_count)
            arrivals[front].append(arrived)
            gather_table = (arrived[None, :] == row_ids[:, None]).astype(jnp.bfloat16)
            summed = jnp.dot(
                gather_table,
                inbound.reshape(slot_count, BR * front_width),
                preferred_element_type=jnp.float32,
            )
            summed = summed.reshape(local_nodes, order_size, front_width)
            upcoming = right_sides[height + 1]
            residual_list[front] = upcoming - summed
    answer = [[None] * levels]
    for height in range(levels - 1, -1, -1):
        front = 0
        if height == levels - 1:
            carried = lower_sols[front][height]
        else:
            destination, source, slot_code = routes[height]
            above_rows = (
                answer[front][height + 1].astype(jnp.bfloat16).reshape(local_rows, BR * front_width)
            )
            arrived = arrivals[front][height]
            outbound = jnp.where(
                (arrived >= 0)[:, None],
                above_rows[jnp.maximum(arrived, 0)],
                jnp.zeros((), jnp.bfloat16),
            )
            outbound = outbound.reshape(devices, capacity, BR * front_width)
            returned = lax.all_to_all(outbound, "snode", split_axis=0, concat_axis=0, tiled=True)
            block_rows = returned.reshape(slot_count, BR * front_width)[destination]
            block_rows = block_rows.reshape(local_nodes, per_node * BR, front_width)
            carried = lower_sols[front][height] - jnp.einsum(
                "skw,skr->swr", off_diagonal[height], block_rows, preferred_element_type=jnp.float32
            )
        result = jnp.einsum("swv,swr->svr", full_diag[height], carried, precision=precise)
        answer[front][height] = result
    stacked = [answer[0][height] for height in range(levels)]
    return jnp.stack(stacked, axis=0)


MESH = pl.DeviceIdType.MESH
PAIR = 2


def mm(a, b):
    return jnp.dot(a, b, preferred_element_type=jnp.float32)


def split(a):
    high = a.astype(jnp.bfloat16)
    return high, (a - high.astype(jnp.float32)).astype(jnp.bfloat16)


def mm3(a_high, a_low, b):
    cols = b.shape[1]
    b_high, b_low = split(b)
    wide = mm(a_high, jnp.concatenate([b_high, b_low], axis=1))
    return wide[:, :cols] + wide[:, cols:] + mm(a_low, b_high)


def dense_kernel(
    n, parts, rs_hbm, dg_ref, od_hbm, snode_v, block_v, snode_s, block_s, out_hbm,
    full, diag_t, od_ref, od_t, rs_ref, low, sol, upd, nat, part, rx, ru, rd, zs, above, picked,
    lsend, osend, dsend, drecv, xsend, xrecv, zsend, urecv, wrecv, asend, arecv, bsend, brecv,
):
    levels, local, order, cols = rs_ref.shape
    per_node = snode_v.shape[2]
    outgoing = local * per_node
    row_blocks = order // BR
    local_rows = local * row_blocks
    line = n // PAIR
    ymany = parts // PAIR
    cut = local
    width = BR // cut
    me = lax.axis_index("snode")
    z, x = me // PAIR, me % PAIR
    mine = lax.axis_index("rhs")
    yy, cc = mine // PAIR, mine % PAIR
    mate = {"snode": z * PAIR + (1 - x)}
    over = {"snode": (z + 1) * PAIR + x}
    under = {"snode": (z - 1) * PAIR + x}
    twin = {"rhs": yy * PAIR + (1 - cc)}
    sides = [(yy + k) % ymany for k in range(1, ymany)]

    def remote(src, dst, s_sem, r_sem, where):
        return pltpu.make_async_remote_copy(
            src_ref=src, dst_ref=dst, send_sem=s_sem, recv_sem=r_sem,
            device_id=where, device_id_type=MESH,
        )

    barrier = pltpu.get_barrier_semaphore()

    def greet(where):
        pl.semaphore_signal(barrier, inc=1, device_id=where, device_id_type=MESH)

    greet(mate)
    greet(twin)
    for side in sides:
        greet({"rhs": side * PAIR + cc})

    @pl.when(z > 0)
    def _():
        greet(under)

    @pl.when(z < line - 1)
    def _():
        greet(over)

    own_diag = [
        pltpu.make_async_copy(dg_ref.at[h], full.at[h, mine], lsend.at[0, h])
        for h in range(levels)
    ]
    load_rs = [
        pltpu.make_async_copy(rs_hbm.at[h], rs_ref.at[h], lsend.at[1, h]) for h in range(levels)
    ]
    load_od = [
        pltpu.make_async_copy(od_hbm.at[h], od_ref.at[h], lsend.at[2, h])
        for h in range(levels - 1)
    ]
    for h in range(levels):
        own_diag[h].start()
        load_rs[h].start()
        if h < levels - 1:
            load_od[h].start()

    ends = jnp.where(z > 0, 1, 0) + jnp.where(z < line - 1, 1, 0)
    pl.semaphore_wait(barrier, 1 + ymany + ends)

    sent = []

    def start_gather(h):
        near = []
        for k, side in enumerate(sides):
            copy = remote(dg_ref.at[h], full.at[h, mine], dsend.at[h, k], drecv.at[h, k],
                          {"rhs": side * PAIR + cc})
            copy.start()
            near.append(copy)
        own = remote(dg_ref.at[h], full.at[h, mine], dsend.at[h, ymany], drecv.at[h, ymany], twin)
        own.start()
        return near, own

    def finish_gather(h, near, own):
        hops = []
        for k, copy in enumerate(near):
            copy.wait_recv()
            origin = ((yy + ymany - 1 - k) % ymany) * PAIR + cc
            hop = remote(full.at[h, origin], full.at[h, origin], dsend.at[h, ymany + 1 + k],
                         drecv.at[h, ymany + 1 + k], twin)
            hop.start()
            hops.append(hop)
        own.wait_recv()
        own_diag[h].wait()
        for hop in hops:
            hop.wait_recv()
        sent.extend(near + [own] + hops)

    def diag(h, s):
        return full[h, :, s].reshape(order, order)

    def forward(h, s, residual):
        high, low_part = split(diag(h, s))
        low[h, s] = mm3(high, low_part, residual)

    def backward(h, s, carried):
        sol[h, s] = mm3(diag_t[h, s, 0], diag_t[h, s, 1], carried)

    def prepare(h):
        for s in range(local):
            high, low_part = split(diag(h, s).T)
            diag_t[h, s, 0] = high
            diag_t[h, s, 1] = low_part

    def turn(h):
        for s in range(local):
            od_t[h, s] = od_ref[h, s].T

    def codes(h):
        code = snode_v[h] * row_blocks + block_v[h]
        return jnp.concatenate([code[s:s + 1] for s in range(local)], axis=1)

    def by_line(body):
        for zz in range(line):
            @pl.when(z == zz)
            def _(zz=zz):
                body(zz)

    def x_copy(h, q, d):
        return remote(part.at[h, q, d * PAIR + (1 - x)], rx.at[h, q, d], xsend.at[h, q, d],
                      xrecv.at[h, q, d], mate)

    def up_copy(h, q, d, where):
        return remote(zs.at[h, q, d], ru.at[h, q, d], zsend.at[h, q, d], urecv.at[h, q, d], where)

    def down_copy(h, q, d, where):
        return remote(zs.at[h, q, d], rd.at[h, q, d], zsend.at[h, q, d], wrecv.at[h, q, d], where)

    def far_first(zz):
        return sorted(range(line), key=lambda d: -abs(d - zz))

    first = start_gather(0)
    tables = []
    rows = lax.broadcasted_iota(jnp.int32, (n * local_rows, outgoing), 0)
    for h in range(levels - 1):
        tables.append(jnp.where(rows == codes(h), 1.0, 0.0).astype(jnp.bfloat16))
    finish_gather(0, *first)
    gather = [None] + [start_gather(h) for h in range(1, levels)]
    load_rs[0].wait()
    for s in range(local):
        forward(0, s, rs_ref[0, s])

    for h in range(levels - 1):
        load_od[h].wait()
        for s in range(local):
            upd[pl.ds(s * per_node * BR, per_node * BR), :] = mm(
                od_ref[h, s], low[h, s].astype(jnp.bfloat16)
            )
        for q in range(cut):
            for r in range(width):
                piece = upd[pl.ds(q * width + r, outgoing, stride=BR), :].astype(jnp.bfloat16)
                summed = mm(tables[h], piece).astype(jnp.bfloat16)
                for d in range(n):
                    part[h, q, d, r * local_rows:(r + 1) * local_rows, :] = (
                        summed[d * local_rows:(d + 1) * local_rows]
                    )

            def send_x(zz, q=q, h=h):
                for d in far_first(zz):
                    x_copy(h, q, d).start()

            by_line(send_x)

        if h == 0:
            prepare(0)
            turn(0)
        if h == levels - 2:
            for later in range(max(h + 1, 2), levels):
                finish_gather(later, *gather[later])
                prepare(later)

        for q in range(cut):
            def reduce(zz, q=q, h=h):
                for d in far_first(zz):
                    x_copy(h, q, d).wait_recv()
                    total = (part[h, q, d * PAIR + x].astype(jnp.float32)
                             + rx[h, q, d].astype(jnp.float32))
                    if d >= zz and zz > 0:
                        up_copy(h, q, d, under).wait_recv()
                        total = total + ru[h, q, d].astype(jnp.float32)
                    if d <= zz and zz < line - 1:
                        down_copy(h, q, d, over).wait_recv()
                        total = total + rd[h, q, d].astype(jnp.float32)
                    if d != zz:
                        zs[h, q, d] = total.astype(jnp.bfloat16)
                    if d > zz:
                        up_copy(h, q, d, over).start()
                    elif d < zz:
                        down_copy(h, q, d, under).start()
                    else:
                        for r in range(width):
                            nat[pl.ds(q * width + r, local_rows, stride=BR), :] = (
                                total[r * local_rows:(r + 1) * local_rows]
                            )

            by_line(reduce)
            if h == 0 and q == 0:
                finish_gather(1, *gather[1])
        load_rs[h + 1].wait()
        for s in range(local):
            forward(h + 1, s, rs_ref[h + 1, s] - nat[pl.ds(s * order, order), :])

    stores = []

    def store(h):
        copy = pltpu.make_async_copy(sol.at[h], out_hbm.at[h], osend.at[h])
        copy.start()
        stores.append(copy)

    def hop(h, q, s, where, s_sem, r_sem, col):
        slot = above[h].at[s * PAIR + col, pl.ds(q * row_blocks, row_blocks)]
        return remote(slot, slot, s_sem, r_sem, where)

    def line_hop(h, q, s, where, way):
        return hop(h, q, s, where, asend.at[h, way, q, s], arecv.at[h, q, s], x)

    def mate_hop(h, q, s, col):
        return hop(h, q, s, mate, bsend.at[h, q, s], brecv.at[h, q, s], col)

    def pass_on(h, q, s, zz):
        if s <= zz and zz < line - 1:
            line_hop(h, q, s, over, 0).start()
        if s >= zz and zz > 0:
            line_hop(h, q, s, under, 1).start()
        mate_hop(h, q, s, x).start()

    def publish(h, q):
        above[h][me, q * row_blocks:(q + 1) * row_blocks] = (
            sol[h + 1, q].reshape(row_blocks, BR, cols).astype(jnp.bfloat16)
        )
        by_line(lambda zz: pass_on(h, q, zz, zz))

    for s in range(local):
        backward(levels - 1, s, low[levels - 1, s])
        publish(levels - 2, s)
    store(levels - 1)

    for h in range(levels - 2, -1, -1):
        if h > 0:
            turn(h)
            prepare(h)

        def spread(zz, h=h):
            for s in sorted(range(line), key=lambda s: abs(s - zz)):
                for q in range(cut):
                    if s != zz:
                        line_hop(h, q, s, over, 0).wait_recv()
                        pass_on(h, q, s, zz)

        by_line(spread)
        for s in range(line):
            for q in range(cut):
                mate_hop(h, q, s, 1 - x).wait_recv()
        for s in range(local):
            for k in range(per_node):
                picked[pl.ds((s * per_node + k) * BR, BR), :] = above[h][
                    snode_s[h, s, k] // local,
                    snode_s[h, s, k] % local * row_blocks + block_s[h, s, k],
                ]
            carried = low[h, s] - mm(
                od_t[h, s], picked[pl.ds(s * per_node * BR, per_node * BR), :]
            )
            backward(h, s, carried)
            if h > 0:
                publish(h - 1, s)
        store(h)

    for copy in sent:
        copy.wait_send()
    for h in range(levels - 1):
        for q in range(cut):
            for d in range(line):
                x_copy(h, q, d).wait_send()
                mate_hop(h, q, d, x).wait_send()

    def drain(zz):
        for h in range(levels - 1):
            for q in range(cut):
                for d in range(line):
                    if d != zz:
                        up_copy(h, q, d, mate).wait_send()
                    if d <= zz and zz < line - 1:
                        line_hop(h, q, d, over, 0).wait_send()
                    if d >= zz and zz > 0:
                        line_hop(h, q, d, under, 1).wait_send()

    by_line(drain)
    for copy in stores:
        copy.wait()


def dense_on_device(right_sides, diag_inverse, off_diagonal, target_snode, target_block):
    levels, local, order, cols = right_sides.shape
    n, parts = lax.axis_size("snode"), lax.axis_size("rhs")
    outgoing = local * target_snode.shape[2]
    row_blocks = order // BR
    local_rows = local * row_blocks
    line = n // PAIR
    ymany = parts // PAIR
    cut = local
    piece = (local_rows * BR // cut, cols)
    bf, f32 = jnp.bfloat16, jnp.float32
    steps = levels - 1
    dma = pltpu.SemaphoreType.DMA
    vmem = pl.BlockSpec(memory_space=pltpu.VMEM)
    smem = pl.BlockSpec(memory_space=pltpu.SMEM)
    hbm = pl.BlockSpec(memory_space=pltpu.HBM)
    return pl.pallas_call(
        functools.partial(dense_kernel, n, parts),
        out_shape=jax.ShapeDtypeStruct(right_sides.shape, f32),
        in_specs=[hbm] * 3 + [vmem] * 2 + [smem] * 2,
        out_specs=hbm,
        scratch_shapes=[
            pltpu.VMEM((levels, parts) + diag_inverse.shape[1:], f32),
            pltpu.VMEM((levels, local, 2, order, order), bf),
            pltpu.VMEM(off_diagonal.shape, bf),
            pltpu.VMEM((steps, local, order, off_diagonal.shape[2]), bf),
            pltpu.VMEM(right_sides.shape, f32),
            pltpu.VMEM(right_sides.shape, f32),
            pltpu.VMEM(right_sides.shape, f32),
            pltpu.VMEM((outgoing * BR, cols), f32),
            pltpu.VMEM((local_rows * BR, cols), f32),
            pltpu.VMEM((steps, cut, n) + piece, bf),
            pltpu.VMEM((steps, cut, line) + piece, bf),
            pltpu.VMEM((steps, cut, line) + piece, bf),
            pltpu.VMEM((steps, cut, line) + piece, bf),
            pltpu.VMEM((steps, cut, line) + piece, bf),
            [pltpu.VMEM((n, local_rows, BR, cols), bf)] * steps,
            pltpu.VMEM((outgoing * BR, cols), bf),
            dma((3, levels)),
            dma((levels,)),
            dma((levels, 2 * ymany)),
            dma((levels, 2 * ymany)),
            dma((steps, cut, line)),
            dma((steps, cut, line)),
            dma((steps, cut, line)),
            dma((steps, cut, line)),
            dma((steps, cut, line)),
            dma((steps, 2, cut, line)),
            dma((steps, cut, line)),
            dma((steps, cut, line)),
            dma((steps, cut, line)),
        ],
        compiler_params=pltpu.CompilerParams(
            collective_id=0, has_side_effects=True, vmem_limit_bytes=56 * 1024 * 1024
        ),
    )(right_sides, diag_inverse, off_diagonal, target_snode, target_block, target_snode,
      target_block)


def program(right_sides, diag_inverse, off_diagonal, target_snode, target_block):
    n, parts = lax.axis_size("snode"), lax.axis_size("rhs")
    capacity = 2 * right_sides.shape[1] * target_snode.shape[2] // n
    local_rows = right_sides.shape[1] * right_sides.shape[2] // BR
    dense = (
        capacity >= local_rows
        and n % PAIR == 0
        and parts % PAIR == 0
        and BR % right_sides.shape[1] == 0
    )
    body = dense_on_device if dense else on_device
    return body(right_sides, diag_inverse, off_diagonal, target_snode, target_block)


def solution(mesh):
    in_specs = (
        P(None, "snode", None, "rhs"),
        P(None, "snode", "rhs", None),
        P(None, "snode", None, None),
        P(None, "snode", None),
        P(None, "snode", None),
    )
    out_specs = P(None, "snode", None, "rhs")
    return jax.shard_map(
        program, mesh=mesh, in_specs=in_specs, out_specs=out_specs, check_vma=False
    )
```

```python
import functools

import jax
import jax.numpy as jnp
from jax import lax
from jax.experimental import pallas as pl
from jax.experimental.pallas import tpu as pltpu
from jax.sharding import PartitionSpec as P

BR = 16


def on_device(right_sides, diag_inverse, off_diagonal, target_snode, target_block):
    precise = lax.Precision.HIGHEST
    levels = right_sides.shape[0]
    local_nodes = right_sides.shape[1]
    order_size = right_sides.shape[2]
    columns = right_sides.shape[3]
    per_node = target_snode.shape[2]
    row_blocks = order_size // BR
    devices = lax.axis_size("snode")
    outgoing = local_nodes * per_node
    capacity = 2 * outgoing // devices
    slot_count = devices * capacity
    local_rows = local_nodes * row_blocks
    front_count = 1
    front_width = columns // front_count
    full_diag = [
        lax.all_gather(diag_inverse[height], "rhs", axis=1, tiled=True) for height in range(levels)
    ]
    block_order = lax.iota(jnp.int32, outgoing)
    slot_ids = lax.iota(jnp.int32, slot_count)
    row_ids = lax.iota(jnp.int32, local_rows)
    routes = []
    for height in range(levels - 1):
        flat_target = target_snode[height].reshape(outgoing)
        owner_dev = flat_target // local_nodes
        target_code = flat_target % local_nodes * row_blocks + target_block[height].reshape(
            outgoing
        )
        earlier = (owner_dev[:, None] == owner_dev[None, :]) & (
            block_order[None, :] < block_order[:, None]
        )
        destination = owner_dev * capacity + jnp.sum(earlier.astype(jnp.int32), axis=1)
        placed = destination[None, :] == slot_ids[:, None]
        source = jnp.max(jnp.where(placed, block_order[None, :], -1), axis=1)
        slot_code = jnp.max(jnp.where(placed, target_code[None, :], -1), axis=1).reshape(
            devices, capacity
        )
        routes.append((destination, source, slot_code))
    residual_list = [right_sides[0]]
    lower_sols = [[]]
    arrivals = [[]]
    for height in range(levels):
        front = 0
        solve_result = jnp.einsum(
            "svw,swr->svr", full_diag[height], residual_list[front], precision=precise
        )
        lower_sols[front].append(solve_result)
        if height + 1 < levels:
            destination, source, slot_code = routes[height]
            update = jnp.einsum(
                "skw,swr->skr",
                off_diagonal[height],
                solve_result.astype(jnp.bfloat16),
                preferred_element_type=jnp.float32,
            )
            update = update.astype(jnp.bfloat16).reshape(outgoing, BR * front_width)
            outbound = jnp.where(
                (source >= 0)[:, None], update[jnp.maximum(source, 0)], jnp.zeros((), jnp.bfloat16)
            )
            outbound = outbound.reshape(devices, capacity, BR * front_width)
            inbound, inbound_code = (
                lax.all_to_all(outbound, "snode", split_axis=0, concat_axis=0, tiled=True),
                lax.all_to_all(slot_code, "snode", split_axis=0, concat_axis=0, tiled=True),
            )
            arrived = inbound_code.reshape(slot_count)
            arrivals[front].append(arrived)
            gather_table = (arrived[None, :] == row_ids[:, None]).astype(jnp.bfloat16)
            summed = jnp.dot(
                gather_table,
                inbound.reshape(slot_count, BR * front_width),
                preferred_element_type=jnp.float32,
            )
            summed = summed.reshape(local_nodes, order_size, front_width)
            upcoming = right_sides[height + 1]
            residual_list[front] = upcoming - summed
    answer = [[None] * levels]
    for height in range(levels - 1, -1, -1):
        front = 0
        if height == levels - 1:
            carried = lower_sols[front][height]
        else:
            destination, source, slot_code = routes[height]
            above_rows = (
                answer[front][height + 1].astype(jnp.bfloat16).reshape(local_rows, BR * front_width)
            )
            arrived = arrivals[front][height]
            outbound = jnp.where(
                (arrived >= 0)[:, None],
                above_rows[jnp.maximum(arrived, 0)],
                jnp.zeros((), jnp.bfloat16),
            )
            outbound = outbound.reshape(devices, capacity, BR * front_width)
            returned = lax.all_to_all(outbound, "snode", split_axis=0, concat_axis=0, tiled=True)
            block_rows = returned.reshape(slot_count, BR * front_width)[destination]
            block_rows = block_rows.reshape(local_nodes, per_node * BR, front_width)
            carried = lower_sols[front][height] - jnp.einsum(
                "skw,skr->swr", off_diagonal[height], block_rows, preferred_element_type=jnp.float32
            )
        result = jnp.einsum("swv,swr->svr", full_diag[height], carried, precision=precise)
        answer[front][height] = result
    stacked = [answer[0][height] for height in range(levels)]
    return jnp.stack(stacked, axis=0)


MESH = pl.DeviceIdType.MESH
PAIR = 2


def mm(a, b):
    return jnp.dot(a, b, preferred_element_type=jnp.float32)


def split(a):
    high = a.astype(jnp.bfloat16)
    return high, (a - high.astype(jnp.float32)).astype(jnp.bfloat16)


def mm3(a_high, a_low, b):
    cols = b.shape[1]
    b_high, b_low = split(b)
    wide = mm(a_high, jnp.concatenate([b_high, b_low], axis=1))
    return wide[:, :cols] + wide[:, cols:] + mm(a_low, b_high)


def dense_kernel(
    n, parts, rs_hbm, dg_ref, od_hbm, snode_v, block_v, snode_s, block_s, out_ref,
    full, diag_t, od_ref, od_t, rs_ref, low, upd, nat, part, rx, rz, zs, above, picked,
    lsend, dsend, drecv, xsend, xrecv, zsend, zrecv, asend, arecv, bsend, brecv,
):
    levels, local, order, cols = rs_ref.shape
    per_node = snode_v.shape[2]
    outgoing = local * per_node
    row_blocks = order // BR
    local_rows = local * row_blocks
    line = n // PAIR
    ymany = parts // PAIR
    cut = local
    width = BR // cut
    me = lax.axis_index("snode")
    z, x = me // PAIR, me % PAIR
    mine = lax.axis_index("rhs")
    yy, cc = mine // PAIR, mine % PAIR
    mate = {"snode": z * PAIR + (1 - x)}
    away = [k for k in (2, 1) if k < line] + list(range(3, line))
    peers = {k: {"snode": (z + k) % line * PAIR + x} for k in away}
    twin = {"rhs": yy * PAIR + (1 - cc)}
    sides = [(yy + k) % ymany for k in range(1, ymany)]

    def remote(src, dst, s_sem, r_sem, where):
        return pltpu.make_async_remote_copy(
            src_ref=src, dst_ref=dst, send_sem=s_sem, recv_sem=r_sem,
            device_id=where, device_id_type=MESH,
        )

    barrier = pltpu.get_barrier_semaphore()

    def greet(where):
        pl.semaphore_signal(barrier, inc=1, device_id=where, device_id_type=MESH)

    greet(mate)
    greet(twin)
    for side in sides:
        greet({"rhs": side * PAIR + cc})

    for k in away:
        greet(peers[k])

    own_diag = [
        pltpu.make_async_copy(dg_ref.at[h], full.at[h, mine], lsend.at[0, h])
        for h in range(levels)
    ]
    load_rs = [
        pltpu.make_async_copy(rs_hbm.at[h], rs_ref.at[h], lsend.at[1, h]) for h in range(levels)
    ]
    load_od = [
        pltpu.make_async_copy(od_hbm.at[h], od_ref.at[h], lsend.at[2, h])
        for h in range(levels - 1)
    ]
    for h in range(levels):
        own_diag[h].start()
        load_rs[h].start()
        if h < levels - 1:
            load_od[h].start()

    pl.semaphore_wait(barrier, ymany + line)

    sent = []

    def start_gather(h):
        near = []
        for k, side in enumerate(sides):
            copy = remote(dg_ref.at[h], full.at[h, mine], dsend.at[h, k], drecv.at[h, k],
                          {"rhs": side * PAIR + cc})
            copy.start()
            near.append(copy)
        own = remote(dg_ref.at[h], full.at[h, mine], dsend.at[h, ymany], drecv.at[h, ymany], twin)
        own.start()
        return near, own

    def finish_gather(h, near, own):
        hops = []
        for k, copy in enumerate(near):
            copy.wait_recv()
            origin = ((yy + ymany - 1 - k) % ymany) * PAIR + cc
            hop = remote(full.at[h, origin], full.at[h, origin], dsend.at[h, ymany + 1 + k],
                         drecv.at[h, ymany + 1 + k], twin)
            hop.start()
            hops.append(hop)
        own.wait_recv()
        own_diag[h].wait()
        for hop in hops:
            hop.wait_recv()
        sent.extend(near + [own] + hops)

    def diag(h, s):
        return full[h, :, s].reshape(order, order)

    def forward(h, s, residual):
        high, low_part = split(diag(h, s))
        low[h, s] = mm3(high, low_part, residual)

    def backward(h, s, carried):
        out_ref[h, s] = mm3(diag_t[h, s, 0], diag_t[h, s, 1], carried)

    def prepare(h):
        for s in range(local):
            high, low_part = split(diag(h, s).T)
            diag_t[h, s, 0] = high
            diag_t[h, s, 1] = low_part

    def turn(h):
        for s in range(local):
            od_t[h, s] = od_ref[h, s].T

    def codes(h):
        code = snode_v[h] * row_blocks + block_v[h]
        return jnp.concatenate([code[s:s + 1] for s in range(local)], axis=1)

    def x_copy(h, q, k):
        d = (z + k) % line
        return remote(part.at[h, q, d * PAIR + (1 - x)], rx.at[h, q, k], xsend.at[h, q, k],
                      xrecv.at[h, q, k], mate)

    def z_copy(h, q, k):
        return remote(zs.at[h, q, k], rz.at[h, q, k], zsend.at[h, q, k], zrecv.at[h, q, k], peers[k])

    first = start_gather(0)
    tables = []
    rows = lax.broadcasted_iota(jnp.int32, (n * local_rows, outgoing), 0)
    for h in range(levels - 1):
        tables.append(jnp.where(rows == codes(h), 1.0, 0.0).astype(jnp.bfloat16))
    finish_gather(0, *first)
    gather = [None] + [start_gather(h) for h in range(1, levels)]
    load_rs[0].wait()
    for s in range(local):
        forward(0, s, rs_ref[0, s])

    for h in range(levels - 1):
        load_od[h].wait()
        for s in range(local):
            upd[pl.ds(s * per_node * BR, per_node * BR), :] = mm(
                od_ref[h, s], low[h, s].astype(jnp.bfloat16)
            )
        for q in range(cut):
            for r in range(width):
                piece = upd[pl.ds(q * width + r, outgoing, stride=BR), :].astype(jnp.bfloat16)
                summed = mm(tables[h], piece).astype(jnp.bfloat16)
                for d in range(n):
                    part[h, q, d, r * local_rows:(r + 1) * local_rows, :] = (
                        summed[d * local_rows:(d + 1) * local_rows]
                    )

            for k in away + [0]:
                x_copy(h, q, k).start()

        if h == 0:
            prepare(0)
            turn(0)
        if h == levels - 2:
            for later in range(max(h + 1, 2), levels):
                finish_gather(later, *gather[later])
                prepare(later)

        def paired(q, k):
            x_copy(h, q, k).wait_recv()
            own = part[h, q, (z + k) % line * PAIR + x]
            return own.astype(jnp.float32) + rx[h, q, k].astype(jnp.float32)

        for q in range(cut):
            for k in away:
                zs[h, q, k] = paired(q, k).astype(jnp.bfloat16)
                z_copy(h, q, k).start()
        if h == 0:
            finish_gather(1, *gather[1])
        for q in range(cut):
            total = paired(q, 0)
            for k in away:
                z_copy(h, q, k).wait_recv()
                total = total + rz[h, q, k].astype(jnp.float32)
            for r in range(width):
                nat[pl.ds(q * width + r, local_rows, stride=BR), :] = (
                    total[r * local_rows:(r + 1) * local_rows]
                )
        load_rs[h + 1].wait()
        for s in range(local):
            forward(h + 1, s, rs_ref[h + 1, s] - nat[pl.ds(s * order, order), :])

    def hop(h, q, source, where, s_sem, r_sem, col):
        slot = above[h].at[source * PAIR + col, pl.ds(q * row_blocks, row_blocks)]
        return remote(slot, slot, s_sem, r_sem, where)

    def line_hop(h, q, k, source):
        return hop(h, q, source, peers[k], asend.at[h, q, k], arecv.at[h, q, k], x)

    def mate_hop(h, q, k, col):
        source = (z + line - k) % line
        return hop(h, q, source, mate, bsend.at[h, q, k], brecv.at[h, q, k], col)

    def publish(h, q):
        above[h][me, q * row_blocks:(q + 1) * row_blocks] = (
            out_ref[h + 1, q].reshape(row_blocks, BR, cols).astype(jnp.bfloat16)
        )
        for k in away:
            line_hop(h, q, k, z).start()
        mate_hop(h, q, 0, x).start()

    for s in range(local):
        backward(levels - 1, s, low[levels - 1, s])
        publish(levels - 2, s)

    for h in range(levels - 2, -1, -1):
        if h > 0:
            turn(h)
            prepare(h)

        for q in range(cut):
            for k in away:
                line_hop(h, q, k, (z + line - k) % line).wait_recv()
                mate_hop(h, q, k, x).start()
        for q in range(cut):
            for k in range(line):
                mate_hop(h, q, k, 1 - x).wait_recv()
        for s in range(local):
            for k in range(per_node):
                picked[pl.ds((s * per_node + k) * BR, BR), :] = above[h][
                    snode_s[h, s, k] // local,
                    snode_s[h, s, k] % local * row_blocks + block_s[h, s, k],
                ]
            carried = low[h, s] - mm(
                od_t[h, s], picked[pl.ds(s * per_node * BR, per_node * BR), :]
            )
            backward(h, s, carried)
            if h > 0:
                publish(h - 1, s)

    for copy in sent:
        copy.wait_send()
    for h in range(levels - 1):
        for q in range(cut):
            for k in range(line):
                x_copy(h, q, k).wait_send()
                mate_hop(h, q, k, x).wait_send()
            for k in away:
                z_copy(h, q, k).wait_send()
                line_hop(h, q, k, z).wait_send()


def dense_on_device(right_sides, diag_inverse, off_diagonal, target_snode, target_block):
    levels, local, order, cols = right_sides.shape
    n, parts = lax.axis_size("snode"), lax.axis_size("rhs")
    outgoing = local * target_snode.shape[2]
    row_blocks = order // BR
    local_rows = local * row_blocks
    line = n // PAIR
    ymany = parts // PAIR
    cut = local
    piece = (local_rows * BR // cut, cols)
    bf, f32 = jnp.bfloat16, jnp.float32
    steps = levels - 1
    dma = pltpu.SemaphoreType.DMA
    vmem = pl.BlockSpec(memory_space=pltpu.VMEM)
    smem = pl.BlockSpec(memory_space=pltpu.SMEM)
    hbm = pl.BlockSpec(memory_space=pltpu.HBM)
    return pl.pallas_call(
        functools.partial(dense_kernel, n, parts),
        out_shape=jax.ShapeDtypeStruct(right_sides.shape, f32),
        in_specs=[hbm] * 3 + [vmem] * 2 + [smem] * 2,
        out_specs=vmem,
        scratch_shapes=[
            pltpu.VMEM((levels, parts) + diag_inverse.shape[1:], f32),
            pltpu.VMEM((levels, local, 2, order, order), bf),
            pltpu.VMEM(off_diagonal.shape, bf),
            pltpu.VMEM((steps, local, order, off_diagonal.shape[2]), bf),
            pltpu.VMEM(right_sides.shape, f32),
            pltpu.VMEM(right_sides.shape, f32),
            pltpu.VMEM((outgoing * BR, cols), f32),
            pltpu.VMEM((local_rows * BR, cols), f32),
            pltpu.VMEM((steps, cut, n) + piece, bf),
            pltpu.VMEM((steps, cut, line) + piece, bf),
            pltpu.VMEM((steps, cut, line) + piece, bf),
            pltpu.VMEM((steps, cut, line) + piece, bf),
            [pltpu.VMEM((n, local_rows, BR, cols), bf)] * steps,
            pltpu.VMEM((outgoing * BR, cols), bf),
            dma((3, levels)),
            dma((levels, 2 * ymany)),
            dma((levels, 2 * ymany)),
            dma((steps, cut, line)),
            dma((steps, cut, line)),
            dma((steps, cut, line)),
            dma((steps, cut, line)),
            dma((steps, cut, line)),
            dma((steps, cut, line)),
            dma((steps, cut, line)),
            dma((steps, cut, line)),
        ],
        compiler_params=pltpu.CompilerParams(
            collective_id=0, has_side_effects=True, vmem_limit_bytes=56 * 1024 * 1024
        ),
    )(right_sides, diag_inverse, off_diagonal, target_snode, target_block, target_snode,
      target_block)


def program(right_sides, diag_inverse, off_diagonal, target_snode, target_block):
    n, parts = lax.axis_size("snode"), lax.axis_size("rhs")
    capacity = 2 * right_sides.shape[1] * target_snode.shape[2] // n
    local_rows = right_sides.shape[1] * right_sides.shape[2] // BR
    dense = (
        capacity >= local_rows
        and n % PAIR == 0
        and parts % PAIR == 0
        and BR % right_sides.shape[1] == 0
    )
    body = dense_on_device if dense else on_device
    return body(right_sides, diag_inverse, off_diagonal, target_snode, target_block)


def solution(mesh):
    in_specs = (
        P(None, "snode", None, "rhs"),
        P(None, "snode", "rhs", None),
        P(None, "snode", None, None),
        P(None, "snode", None),
        P(None, "snode", None),
    )
    out_specs = P(None, "snode", None, "rhs")
    return jax.shard_map(
        program, mesh=mesh, in_specs=in_specs, out_specs=out_specs, check_vma=False
    )
```

```python
import functools

import jax
import jax.numpy as jnp
from jax import lax
from jax.experimental import pallas as pl
from jax.experimental.pallas import tpu as pltpu
from jax.sharding import PartitionSpec as P

BR = 16


def on_device(right_sides, diag_inverse, off_diagonal, target_snode, target_block):
    precise = lax.Precision.HIGHEST
    levels = right_sides.shape[0]
    local_nodes = right_sides.shape[1]
    order_size = right_sides.shape[2]
    columns = right_sides.shape[3]
    per_node = target_snode.shape[2]
    row_blocks = order_size // BR
    devices = lax.axis_size("snode")
    outgoing = local_nodes * per_node
    capacity = 2 * outgoing // devices
    slot_count = devices * capacity
    local_rows = local_nodes * row_blocks
    front_count = 1
    front_width = columns // front_count
    full_diag = [
        lax.all_gather(diag_inverse[height], "rhs", axis=1, tiled=True) for height in range(levels)
    ]
    block_order = lax.iota(jnp.int32, outgoing)
    slot_ids = lax.iota(jnp.int32, slot_count)
    row_ids = lax.iota(jnp.int32, local_rows)
    routes = []
    for height in range(levels - 1):
        flat_target = target_snode[height].reshape(outgoing)
        owner_dev = flat_target // local_nodes
        target_code = flat_target % local_nodes * row_blocks + target_block[height].reshape(
            outgoing
        )
        earlier = (owner_dev[:, None] == owner_dev[None, :]) & (
            block_order[None, :] < block_order[:, None]
        )
        destination = owner_dev * capacity + jnp.sum(earlier.astype(jnp.int32), axis=1)
        placed = destination[None, :] == slot_ids[:, None]
        source = jnp.max(jnp.where(placed, block_order[None, :], -1), axis=1)
        slot_code = jnp.max(jnp.where(placed, target_code[None, :], -1), axis=1).reshape(
            devices, capacity
        )
        routes.append((destination, source, slot_code))
    residual_list = [right_sides[0]]
    lower_sols = [[]]
    arrivals = [[]]
    for height in range(levels):
        front = 0
        solve_result = jnp.einsum(
            "svw,swr->svr", full_diag[height], residual_list[front], precision=precise
        )
        lower_sols[front].append(solve_result)
        if height + 1 < levels:
            destination, source, slot_code = routes[height]
            update = jnp.einsum(
                "skw,swr->skr",
                off_diagonal[height],
                solve_result.astype(jnp.bfloat16),
                preferred_element_type=jnp.float32,
            )
            update = update.astype(jnp.bfloat16).reshape(outgoing, BR * front_width)
            outbound = jnp.where(
                (source >= 0)[:, None], update[jnp.maximum(source, 0)], jnp.zeros((), jnp.bfloat16)
            )
            outbound = outbound.reshape(devices, capacity, BR * front_width)
            inbound, inbound_code = (
                lax.all_to_all(outbound, "snode", split_axis=0, concat_axis=0, tiled=True),
                lax.all_to_all(slot_code, "snode", split_axis=0, concat_axis=0, tiled=True),
            )
            arrived = inbound_code.reshape(slot_count)
            arrivals[front].append(arrived)
            gather_table = (arrived[None, :] == row_ids[:, None]).astype(jnp.bfloat16)
            summed = jnp.dot(
                gather_table,
                inbound.reshape(slot_count, BR * front_width),
                preferred_element_type=jnp.float32,
            )
            summed = summed.reshape(local_nodes, order_size, front_width)
            upcoming = right_sides[height + 1]
            residual_list[front] = upcoming - summed
    answer = [[None] * levels]
    for height in range(levels - 1, -1, -1):
        front = 0
        if height == levels - 1:
            carried = lower_sols[front][height]
        else:
            destination, source, slot_code = routes[height]
            above_rows = (
                answer[front][height + 1].astype(jnp.bfloat16).reshape(local_rows, BR * front_width)
            )
            arrived = arrivals[front][height]
            outbound = jnp.where(
                (arrived >= 0)[:, None],
                above_rows[jnp.maximum(arrived, 0)],
                jnp.zeros((), jnp.bfloat16),
            )
            outbound = outbound.reshape(devices, capacity, BR * front_width)
            returned = lax.all_to_all(outbound, "snode", split_axis=0, concat_axis=0, tiled=True)
            block_rows = returned.reshape(slot_count, BR * front_width)[destination]
            block_rows = block_rows.reshape(local_nodes, per_node * BR, front_width)
            carried = lower_sols[front][height] - jnp.einsum(
                "skw,skr->swr", off_diagonal[height], block_rows, preferred_element_type=jnp.float32
            )
        result = jnp.einsum("swv,swr->svr", full_diag[height], carried, precision=precise)
        answer[front][height] = result
    stacked = [answer[0][height] for height in range(levels)]
    return jnp.stack(stacked, axis=0)


MESH = pl.DeviceIdType.MESH
PAIR = 2


def mm(a, b):
    return jnp.dot(a, b, preferred_element_type=jnp.float32)


def split(a):
    high = a.astype(jnp.bfloat16)
    return high, (a - high.astype(jnp.float32)).astype(jnp.bfloat16)


def mm3(a_high, a_low, b):
    cols = b.shape[1]
    b_high, b_low = split(b)
    wide = mm(a_high, jnp.concatenate([b_high, b_low], axis=1))
    return wide[:, :cols] + wide[:, cols:] + mm(a_low, b_high)


def dense_kernel(
    n, parts, rs_hbm, dg_ref, od_hbm, snode_v, block_v, snode_s, block_s, out_ref,
    full, diag_t, od_ref, od_t, rs_ref, low, upd, nat, part, rx, rz, zs, above, picked,
    lsend, dsend, drecv, xsend, xrecv, zsend, zrecv, asend, arecv, bsend, brecv,
):
    levels, local, order, cols = rs_ref.shape
    per_node = snode_v.shape[2]
    outgoing = local * per_node
    row_blocks = order // BR
    local_rows = local * row_blocks
    line = n // PAIR
    ymany = parts // PAIR
    cut = local
    width = BR // cut
    me = lax.axis_index("snode")
    z, x = me // PAIR, me % PAIR
    mine = lax.axis_index("rhs")
    yy, cc = mine // PAIR, mine % PAIR
    mate = {"snode": z * PAIR + (1 - x)}
    away = [k for k in (2, 1) if k < line] + list(range(3, line))
    peers = {k: {"snode": (z + k) % line * PAIR + x} for k in away}
    twin = {"rhs": yy * PAIR + (1 - cc)}
    sides = [(yy + k) % ymany for k in range(1, ymany)]

    def remote(src, dst, s_sem, r_sem, where):
        return pltpu.make_async_remote_copy(
            src_ref=src, dst_ref=dst, send_sem=s_sem, recv_sem=r_sem,
            device_id=where, device_id_type=MESH,
        )

    barrier = pltpu.get_barrier_semaphore()

    def greet(where):
        pl.semaphore_signal(barrier, inc=1, device_id=where, device_id_type=MESH)

    greet(mate)
    greet(twin)
    for side in sides:
        greet({"rhs": side * PAIR + cc})

    for k in away:
        greet(peers[k])

    own_diag = [
        pltpu.make_async_copy(dg_ref.at[h], full.at[h, mine], lsend.at[0, h])
        for h in range(levels)
    ]
    load_rs = [
        pltpu.make_async_copy(rs_hbm.at[h], rs_ref.at[h], lsend.at[1, h]) for h in range(levels)
    ]
    load_od = [
        pltpu.make_async_copy(od_hbm.at[h], od_ref.at[h], lsend.at[2, h])
        for h in range(levels - 1)
    ]
    for h in range(levels):
        own_diag[h].start()
        load_rs[h].start()
        if h < levels - 1:
            load_od[h].start()

    pl.semaphore_wait(barrier, ymany + line)

    sent = []

    def start_gather(h):
        near = []
        for k, side in enumerate(sides):
            copy = remote(dg_ref.at[h], full.at[h, mine], dsend.at[h, k], drecv.at[h, k],
                          {"rhs": side * PAIR + cc})
            copy.start()
            near.append(copy)
        own = remote(dg_ref.at[h], full.at[h, mine], dsend.at[h, ymany], drecv.at[h, ymany], twin)
        own.start()
        return near, own

    def finish_gather(h, near, own, meanwhile=None):
        hops = []
        for k, copy in enumerate(near):
            copy.wait_recv()
            origin = ((yy + ymany - 1 - k) % ymany) * PAIR + cc
            hop = remote(full.at[h, origin], full.at[h, origin], dsend.at[h, ymany + 1 + k],
                         drecv.at[h, ymany + 1 + k], twin)
            hop.start()
            hops.append(hop)
        if meanwhile is not None:
            meanwhile()
        own.wait_recv()
        own_diag[h].wait()
        for hop in hops:
            hop.wait_recv()
        sent.extend(near + [own] + hops)

    def diag(h, s):
        return full[h, :, s].reshape(order, order)

    def forward(h, s, residual):
        high, low_part = split(diag(h, s))
        low[h, s] = mm3(high, low_part, residual)

    def backward(h, s, carried):
        out_ref[h, s] = mm3(diag_t[h, s, 0], diag_t[h, s, 1], carried)

    def prepare(h):
        for s in range(local):
            high, low_part = split(diag(h, s).T)
            diag_t[h, s, 0] = high
            diag_t[h, s, 1] = low_part

    def turn(h):
        for s in range(local):
            od_t[h, s] = od_ref[h, s].T

    def codes(h):
        code = snode_v[h] * row_blocks + block_v[h]
        return jnp.concatenate([code[s:s + 1] for s in range(local)], axis=1)

    def x_copy(h, q, k):
        d = (z + k) % line
        return remote(part.at[h, q, d * PAIR + (1 - x)], rx.at[h, q, k], xsend.at[h, q, k],
                      xrecv.at[h, q, k], mate)

    def z_copy(h, q, k):
        return remote(zs.at[h, q, k], rz.at[h, q, k], zsend.at[h, q, k], zrecv.at[h, q, k], peers[k])

    first = start_gather(0)
    tables = []
    rows = lax.broadcasted_iota(jnp.int32, (n * local_rows, outgoing), 0)
    for h in range(levels - 1):
        tables.append(jnp.where(rows == codes(h), 1.0, 0.0).astype(jnp.bfloat16))
    load_od[0].wait()
    turn(0)

    def turn_rest():
        for h in range(1, levels - 1):
            load_od[h].wait()
            turn(h)

    finish_gather(0, *first, meanwhile=turn_rest)
    gather = [None] + [start_gather(h) for h in range(1, levels)]
    load_rs[0].wait()
    for s in range(local):
        forward(0, s, rs_ref[0, s])

    for h in range(levels - 1):
        for s in range(local):
            upd[pl.ds(s * per_node * BR, per_node * BR), :] = mm(
                od_ref[h, s], low[h, s].astype(jnp.bfloat16)
            )
        for q in range(cut):
            for r in range(width):
                piece = upd[pl.ds(q * width + r, outgoing, stride=BR), :].astype(jnp.bfloat16)
                summed = mm(tables[h], piece).astype(jnp.bfloat16)
                for d in range(n):
                    part[h, q, d, r * local_rows:(r + 1) * local_rows, :] = (
                        summed[d * local_rows:(d + 1) * local_rows]
                    )

            for k in away + [0]:
                x_copy(h, q, k).start()

        def paired(q, k):
            x_copy(h, q, k).wait_recv()
            own = part[h, q, (z + k) % line * PAIR + x]
            return own.astype(jnp.float32) + rx[h, q, k].astype(jnp.float32)

        for q in range(cut):
            for k in away:
                zs[h, q, k] = paired(q, k).astype(jnp.bfloat16)
                z_copy(h, q, k).start()
        prepare(h)
        finish_gather(h + 1, *gather[h + 1])
        if h == levels - 2:
            prepare(levels - 1)
        for q in range(cut):
            total = paired(q, 0)
            for k in away:
                z_copy(h, q, k).wait_recv()
                total = total + rz[h, q, k].astype(jnp.float32)
            for r in range(width):
                nat[pl.ds(q * width + r, local_rows, stride=BR), :] = (
                    total[r * local_rows:(r + 1) * local_rows]
                )
        load_rs[h + 1].wait()
        for s in range(local):
            forward(h + 1, s, rs_ref[h + 1, s] - nat[pl.ds(s * order, order), :])

    def hop(h, q, source, where, s_sem, r_sem, col):
        slot = above[h].at[
            pl.ds(((source * PAIR + col) * local + q) * row_blocks, row_blocks)
        ]
        return remote(slot, slot, s_sem, r_sem, where)

    def line_hop(h, q, k, source):
        return hop(h, q, source, peers[k], asend.at[h, q, k], arecv.at[h, q, k], x)

    def mate_hop(h, q, k, col):
        source = (z + line - k) % line
        return hop(h, q, source, mate, bsend.at[h, q, k], brecv.at[h, q, k], col)

    def publish(h, q):
        above[h][pl.ds((me * local + q) * row_blocks, row_blocks)] = (
            out_ref[h + 1, q].reshape(row_blocks, BR, cols).astype(jnp.bfloat16)
        )
        mate_hop(h, q, 0, x).start()
        for k in away:
            line_hop(h, q, k, z).start()

    for s in range(local):
        backward(levels - 1, s, low[levels - 1, s])
        publish(levels - 2, s)

    for h in range(levels - 2, -1, -1):
        for q in range(cut):
            for k in away:
                line_hop(h, q, k, (z + line - k) % line).wait_recv()
                mate_hop(h, q, k, x).start()
        for q in range(cut):
            for k in range(line):
                mate_hop(h, q, k, 1 - x).wait_recv()
        for s in range(local):
            for k in range(per_node):
                picked[pl.ds((s * per_node + k) * BR, BR), :] = above[h][
                    snode_s[h, s, k] * row_blocks + block_s[h, s, k]
                ]
            carried = low[h, s] - mm(
                od_t[h, s], picked[pl.ds(s * per_node * BR, per_node * BR), :]
            )
            backward(h, s, carried)
            if h > 0:
                publish(h - 1, s)

    for copy in sent:
        copy.wait_send()
    for h in range(levels - 1):
        for q in range(cut):
            for k in range(line):
                x_copy(h, q, k).wait_send()
                mate_hop(h, q, k, x).wait_send()
            for k in away:
                z_copy(h, q, k).wait_send()
                line_hop(h, q, k, z).wait_send()


def dense_on_device(right_sides, diag_inverse, off_diagonal, target_snode, target_block):
    levels, local, order, cols = right_sides.shape
    n, parts = lax.axis_size("snode"), lax.axis_size("rhs")
    outgoing = local * target_snode.shape[2]
    row_blocks = order // BR
    local_rows = local * row_blocks
    line = n // PAIR
    ymany = parts // PAIR
    cut = local
    piece = (local_rows * BR // cut, cols)
    bf, f32 = jnp.bfloat16, jnp.float32
    steps = levels - 1
    dma = pltpu.SemaphoreType.DMA
    vmem = pl.BlockSpec(memory_space=pltpu.VMEM)
    smem = pl.BlockSpec(memory_space=pltpu.SMEM)
    hbm = pl.BlockSpec(memory_space=pltpu.HBM)
    return pl.pallas_call(
        functools.partial(dense_kernel, n, parts),
        out_shape=jax.ShapeDtypeStruct(right_sides.shape, f32),
        in_specs=[hbm] * 3 + [vmem] * 2 + [smem] * 2,
        out_specs=vmem,
        scratch_shapes=[
            pltpu.VMEM((levels, parts) + diag_inverse.shape[1:], f32),
            pltpu.VMEM((levels, local, 2, order, order), bf),
            pltpu.VMEM(off_diagonal.shape, bf),
            pltpu.VMEM((steps, local, order, off_diagonal.shape[2]), bf),
            pltpu.VMEM(right_sides.shape, f32),
            pltpu.VMEM(right_sides.shape, f32),
            pltpu.VMEM((outgoing * BR, cols), f32),
            pltpu.VMEM((local_rows * BR, cols), f32),
            pltpu.VMEM((steps, cut, n) + piece, bf),
            pltpu.VMEM((steps, cut, line) + piece, bf),
            pltpu.VMEM((steps, cut, line) + piece, bf),
            pltpu.VMEM((steps, cut, line) + piece, bf),
            [pltpu.VMEM((n * local_rows, BR, cols), bf)] * steps,
            pltpu.VMEM((outgoing * BR, cols), bf),
            dma((3, levels)),
            dma((levels, 2 * ymany)),
            dma((levels, 2 * ymany)),
            dma((steps, cut, line)),
            dma((steps, cut, line)),
            dma((steps, cut, line)),
            dma((steps, cut, line)),
            dma((steps, cut, line)),
            dma((steps, cut, line)),
            dma((steps, cut, line)),
            dma((steps, cut, line)),
        ],
        compiler_params=pltpu.CompilerParams(
            collective_id=0, has_side_effects=True, vmem_limit_bytes=40 * 1024 * 1024
        ),
    )(right_sides, diag_inverse, off_diagonal, target_snode, target_block, target_snode,
      target_block)


def program(right_sides, diag_inverse, off_diagonal, target_snode, target_block):
    n, parts = lax.axis_size("snode"), lax.axis_size("rhs")
    capacity = 2 * right_sides.shape[1] * target_snode.shape[2] // n
    local_rows = right_sides.shape[1] * right_sides.shape[2] // BR
    dense = (
        capacity >= local_rows
        and n % PAIR == 0
        and parts % PAIR == 0
        and BR % right_sides.shape[1] == 0
    )
    body = dense_on_device if dense else on_device
    return body(right_sides, diag_inverse, off_diagonal, target_snode, target_block)


def solution(mesh):
    in_specs = (
        P(None, "snode", None, "rhs"),
        P(None, "snode", "rhs", None),
        P(None, "snode", None, None),
        P(None, "snode", None),
        P(None, "snode", None),
    )
    out_specs = P(None, "snode", None, "rhs")
    return jax.shard_map(
        program, mesh=mesh, in_specs=in_specs, out_specs=out_specs, check_vma=False
    )
```

```python
import functools

import jax
import jax.numpy as jnp
from jax import lax
from jax.experimental import pallas as pl
from jax.experimental.pallas import tpu as pltpu
from jax.sharding import PartitionSpec as P

BR = 16


def on_device(right_sides, diag_inverse, off_diagonal, target_snode, target_block):
    precise = lax.Precision.HIGHEST
    levels = right_sides.shape[0]
    local_nodes = right_sides.shape[1]
    order_size = right_sides.shape[2]
    columns = right_sides.shape[3]
    per_node = target_snode.shape[2]
    row_blocks = order_size // BR
    devices = lax.axis_size("snode")
    outgoing = local_nodes * per_node
    capacity = 2 * outgoing // devices
    slot_count = devices * capacity
    local_rows = local_nodes * row_blocks
    front_count = 1
    front_width = columns // front_count
    full_diag = [
        lax.all_gather(diag_inverse[height], "rhs", axis=1, tiled=True) for height in range(levels)
    ]
    block_order = lax.iota(jnp.int32, outgoing)
    slot_ids = lax.iota(jnp.int32, slot_count)
    row_ids = lax.iota(jnp.int32, local_rows)
    routes = []
    for height in range(levels - 1):
        flat_target = target_snode[height].reshape(outgoing)
        owner_dev = flat_target // local_nodes
        target_code = flat_target % local_nodes * row_blocks + target_block[height].reshape(
            outgoing
        )
        earlier = (owner_dev[:, None] == owner_dev[None, :]) & (
            block_order[None, :] < block_order[:, None]
        )
        destination = owner_dev * capacity + jnp.sum(earlier.astype(jnp.int32), axis=1)
        placed = destination[None, :] == slot_ids[:, None]
        source = jnp.max(jnp.where(placed, block_order[None, :], -1), axis=1)
        slot_code = jnp.max(jnp.where(placed, target_code[None, :], -1), axis=1).reshape(
            devices, capacity
        )
        routes.append((destination, source, slot_code))
    residual_list = [right_sides[0]]
    lower_sols = [[]]
    arrivals = [[]]
    for height in range(levels):
        front = 0
        solve_result = jnp.einsum(
            "svw,swr->svr", full_diag[height], residual_list[front], precision=precise
        )
        lower_sols[front].append(solve_result)
        if height + 1 < levels:
            destination, source, slot_code = routes[height]
            update = jnp.einsum(
                "skw,swr->skr",
                off_diagonal[height],
                solve_result.astype(jnp.bfloat16),
                preferred_element_type=jnp.float32,
            )
            update = update.astype(jnp.bfloat16).reshape(outgoing, BR * front_width)
            outbound = jnp.where(
                (source >= 0)[:, None], update[jnp.maximum(source, 0)], jnp.zeros((), jnp.bfloat16)
            )
            outbound = outbound.reshape(devices, capacity, BR * front_width)
            inbound, inbound_code = (
                lax.all_to_all(outbound, "snode", split_axis=0, concat_axis=0, tiled=True),
                lax.all_to_all(slot_code, "snode", split_axis=0, concat_axis=0, tiled=True),
            )
            arrived = inbound_code.reshape(slot_count)
            arrivals[front].append(arrived)
            gather_table = (arrived[None, :] == row_ids[:, None]).astype(jnp.bfloat16)
            summed = jnp.dot(
                gather_table,
                inbound.reshape(slot_count, BR * front_width),
                preferred_element_type=jnp.float32,
            )
            summed = summed.reshape(local_nodes, order_size, front_width)
            upcoming = right_sides[height + 1]
            residual_list[front] = upcoming - summed
    answer = [[None] * levels]
    for height in range(levels - 1, -1, -1):
        front = 0
        if height == levels - 1:
            carried = lower_sols[front][height]
        else:
            destination, source, slot_code = routes[height]
            above_rows = (
                answer[front][height + 1].astype(jnp.bfloat16).reshape(local_rows, BR * front_width)
            )
            arrived = arrivals[front][height]
            outbound = jnp.where(
                (arrived >= 0)[:, None],
                above_rows[jnp.maximum(arrived, 0)],
                jnp.zeros((), jnp.bfloat16),
            )
            outbound = outbound.reshape(devices, capacity, BR * front_width)
            returned = lax.all_to_all(outbound, "snode", split_axis=0, concat_axis=0, tiled=True)
            block_rows = returned.reshape(slot_count, BR * front_width)[destination]
            block_rows = block_rows.reshape(local_nodes, per_node * BR, front_width)
            carried = lower_sols[front][height] - jnp.einsum(
                "skw,skr->swr", off_diagonal[height], block_rows, preferred_element_type=jnp.float32
            )
        result = jnp.einsum("swv,swr->svr", full_diag[height], carried, precision=precise)
        answer[front][height] = result
    stacked = [answer[0][height] for height in range(levels)]
    return jnp.stack(stacked, axis=0)


MESH = pl.DeviceIdType.MESH
PAIR = 2


def mm(a, b):
    return jnp.dot(a, b, preferred_element_type=jnp.float32)


def split(a):
    high = a.astype(jnp.bfloat16)
    return high, (a - high.astype(jnp.float32)).astype(jnp.bfloat16)


def mm3(a_high, a_low, b):
    cols = b.shape[1]
    b_high, b_low = split(b)
    wide = mm(a_high, jnp.concatenate([b_high, b_low], axis=1))
    return wide[:, :cols] + wide[:, cols:] + mm(a_low, b_high)


def dense_kernel(
    n, parts, rs_hbm, dg_ref, od_hbm, snode_v, block_v, snode_s, block_s, out_ref,
    full, diag_t, od_ref, od_t, rs_ref, low, upd, nat, part, rx, rz, zs, above, picked,
    lsend, dsend, drecv, xsend, xrecv, zsend, zrecv, asend, arecv, bsend, brecv, token,
):
    levels, local, order, cols = rs_ref.shape
    per_node = snode_v.shape[2]
    outgoing = local * per_node
    row_blocks = order // BR
    local_rows = local * row_blocks
    line = n // PAIR
    ymany = parts // PAIR
    cut = local
    width = BR // cut
    me = lax.axis_index("snode")
    z, x = me // PAIR, me % PAIR
    mine = lax.axis_index("rhs")
    yy, cc = mine // PAIR, mine % PAIR
    mate = {"snode": z * PAIR + (1 - x)}
    away = [k for k in (2, 1) if k < line] + list(range(3, line))
    peers = {k: {"snode": (z + k) % line * PAIR + x} for k in away}
    twin = {"rhs": yy * PAIR + (1 - cc)}
    sides = [(yy + k) % ymany for k in range(1, ymany)]

    def remote(src, dst, s_sem, r_sem, where):
        return pltpu.make_async_remote_copy(
            src_ref=src, dst_ref=dst, send_sem=s_sem, recv_sem=r_sem,
            device_id=where, device_id_type=MESH,
        )

    barrier = pltpu.get_barrier_semaphore()

    def greet(where):
        pl.semaphore_signal(barrier, inc=1, device_id=where, device_id_type=MESH)

    greet(mate)
    greet(twin)
    for side in sides:
        greet({"rhs": side * PAIR + cc})

    for k in away:
        greet(peers[k])

    own_diag = [
        pltpu.make_async_copy(dg_ref.at[h], full.at[h, mine], lsend.at[0, h])
        for h in range(levels)
    ]
    load_rs = [
        pltpu.make_async_copy(rs_hbm.at[h], rs_ref.at[h], lsend.at[1, h]) for h in range(levels)
    ]
    load_od = [
        pltpu.make_async_copy(od_hbm.at[h], od_ref.at[h], lsend.at[2, h])
        for h in range(levels - 1)
    ]
    for h in range(levels):
        own_diag[h].start()
        load_rs[h].start()
        if h < levels - 1:
            load_od[h].start()

    pl.semaphore_wait(barrier, ymany + line)

    sent = []

    def start_gather(h):
        near = []
        for k, side in enumerate(sides):
            copy = remote(dg_ref.at[h], full.at[h, mine], dsend.at[h, k], drecv.at[h, k],
                          {"rhs": side * PAIR + cc})
            copy.start()
            near.append(copy)
        own = remote(dg_ref.at[h], full.at[h, mine], dsend.at[h, ymany], drecv.at[h, ymany], twin)
        own.start()
        return near, own

    def finish_gather(h, near, own, meanwhile=None):
        hops = []
        for k, copy in enumerate(near):
            copy.wait_recv()
            origin = ((yy + ymany - 1 - k) % ymany) * PAIR + cc
            hop = remote(full.at[h, origin], full.at[h, origin], dsend.at[h, ymany + 1 + k],
                         drecv.at[h, ymany + 1 + k], twin)
            hop.start()
            hops.append(hop)
        if meanwhile is not None:
            meanwhile()
        own.wait_recv()
        own_diag[h].wait()
        for hop in hops:
            hop.wait_recv()
        sent.extend(near + [own] + hops)

    def diag(h, s):
        return full[h, :, s].reshape(order, order)

    def forward(h, s, residual):
        high, low_part = split(diag(h, s))
        low[h, s] = mm3(high, low_part, residual)

    def backward(h, s, carried):
        out_ref[h, s] = mm3(diag_t[h, s, 0], diag_t[h, s, 1], carried)

    def prepare(h):
        for s in range(local):
            high, low_part = split(diag(h, s).T)
            diag_t[h, s, 0] = high
            diag_t[h, s, 1] = low_part

    def turn(h):
        for s in range(local):
            od_t[h, s] = od_ref[h, s].T

    def codes(h):
        code = snode_v[h] * row_blocks + block_v[h]
        return jnp.concatenate([code[s:s + 1] for s in range(local)], axis=1)

    def x_copy(h, q, k):
        d = (z + k) % line
        return remote(part.at[h, q, d * PAIR + (1 - x)], rx.at[h, q, k], xsend.at[h, q, k],
                      xrecv.at[h, q, k], mate)

    def z_copy(h, q, k):
        return remote(zs.at[h, q, k], rz.at[h, q, k], zsend.at[h, q, k], zrecv.at[h, q, k], peers[k])

    first = start_gather(0)
    tables = []
    rows = lax.broadcasted_iota(jnp.int32, (n * local_rows, outgoing), 0)
    for h in range(levels - 1):
        tables.append(jnp.where(rows == codes(h), 1.0, 0.0).astype(jnp.bfloat16))
    load_od[0].wait()
    turn(0)

    def turn_rest():
        for h in range(1, levels - 1):
            load_od[h].wait()
            turn(h)

    finish_gather(0, *first, meanwhile=turn_rest)
    gather = [None] + [start_gather(h) for h in range(1, levels)]
    load_rs[0].wait()
    for s in range(local):
        forward(0, s, rs_ref[0, s])

    for h in range(levels - 1):
        for s in range(local):
            upd[pl.ds(s * per_node * BR, per_node * BR), :] = mm(
                od_ref[h, s], low[h, s].astype(jnp.bfloat16)
            )
        for q in range(cut):
            for r in range(width):
                piece = upd[pl.ds(q * width + r, outgoing, stride=BR), :].astype(jnp.bfloat16)
                summed = mm(tables[h], piece).astype(jnp.bfloat16)
                for d in range(n):
                    part[h, q, d, r * local_rows:(r + 1) * local_rows, :] = (
                        summed[d * local_rows:(d + 1) * local_rows]
                    )

            if h == 0 and q == 0:
                @pl.when(cc == 0)
                def _():
                    pl.semaphore_wait(token, 1)

            for k in away + [0]:
                x_copy(h, q, k).start()

        def paired(q, k):
            x_copy(h, q, k).wait_recv()
            own = part[h, q, (z + k) % line * PAIR + x]
            return own.astype(jnp.float32) + rx[h, q, k].astype(jnp.float32)

        for q in range(cut):
            for k in away:
                zs[h, q, k] = paired(q, k).astype(jnp.bfloat16)
                z_copy(h, q, k).start()
        if h == 0:
            for q in range(cut):
                for k in range(line):
                    x_copy(h, q, k).wait_send()

            @pl.when(cc == 1)
            def _():
                pl.semaphore_signal(token, inc=1, device_id=twin, device_id_type=MESH)

        prepare(h)
        finish_gather(h + 1, *gather[h + 1])
        if h == levels - 2:
            prepare(levels - 1)
        for q in range(cut):
            total = paired(q, 0)
            for k in away:
                z_copy(h, q, k).wait_recv()
                total = total + rz[h, q, k].astype(jnp.float32)
            for r in range(width):
                nat[pl.ds(q * width + r, local_rows, stride=BR), :] = (
                    total[r * local_rows:(r + 1) * local_rows]
                )
        load_rs[h + 1].wait()
        for s in range(local):
            forward(h + 1, s, rs_ref[h + 1, s] - nat[pl.ds(s * order, order), :])

    def hop(h, q, source, where, s_sem, r_sem, col):
        slot = above[h].at[
            pl.ds(((source * PAIR + col) * local + q) * row_blocks, row_blocks)
        ]
        return remote(slot, slot, s_sem, r_sem, where)

    def line_hop(h, q, k, source):
        return hop(h, q, source, peers[k], asend.at[h, q, k], arecv.at[h, q, k], x)

    def mate_hop(h, q, k, col):
        source = (z + line - k) % line
        return hop(h, q, source, mate, bsend.at[h, q, k], brecv.at[h, q, k], col)

    def publish(h, q):
        above[h][pl.ds((me * local + q) * row_blocks, row_blocks)] = (
            out_ref[h + 1, q].reshape(row_blocks, BR, cols).astype(jnp.bfloat16)
        )
        mate_hop(h, q, 0, x).start()
        for k in away:
            line_hop(h, q, k, z).start()

    for s in range(local):
        backward(levels - 1, s, low[levels - 1, s])
        publish(levels - 2, s)

    for h in range(levels - 2, -1, -1):
        for q in range(cut):
            for k in away:
                line_hop(h, q, k, (z + line - k) % line).wait_recv()
                mate_hop(h, q, k, x).start()
        for q in range(cut):
            for k in range(line):
                mate_hop(h, q, k, 1 - x).wait_recv()
        for s in range(local):
            for k in range(per_node):
                picked[pl.ds((s * per_node + k) * BR, BR), :] = above[h][
                    snode_s[h, s, k] * row_blocks + block_s[h, s, k]
                ]
            carried = low[h, s] - mm(
                od_t[h, s], picked[pl.ds(s * per_node * BR, per_node * BR), :]
            )
            backward(h, s, carried)
            if h > 0:
                publish(h - 1, s)

    for copy in sent:
        copy.wait_send()
    for h in range(levels - 1):
        for q in range(cut):
            for k in range(line):
                if h > 0:
                    x_copy(h, q, k).wait_send()
                mate_hop(h, q, k, x).wait_send()
            for k in away:
                z_copy(h, q, k).wait_send()
                line_hop(h, q, k, z).wait_send()


def dense_on_device(right_sides, diag_inverse, off_diagonal, target_snode, target_block):
    levels, local, order, cols = right_sides.shape
    n, parts = lax.axis_size("snode"), lax.axis_size("rhs")
    outgoing = local * target_snode.shape[2]
    row_blocks = order // BR
    local_rows = local * row_blocks
    line = n // PAIR
    ymany = parts // PAIR
    cut = local
    piece = (local_rows * BR // cut, cols)
    bf, f32 = jnp.bfloat16, jnp.float32
    steps = levels - 1
    dma = pltpu.SemaphoreType.DMA
    vmem = pl.BlockSpec(memory_space=pltpu.VMEM)
    smem = pl.BlockSpec(memory_space=pltpu.SMEM)
    hbm = pl.BlockSpec(memory_space=pltpu.HBM)
    return pl.pallas_call(
        functools.partial(dense_kernel, n, parts),
        out_shape=jax.ShapeDtypeStruct(right_sides.shape, f32),
        in_specs=[hbm] * 3 + [vmem] * 2 + [smem] * 2,
        out_specs=vmem,
        scratch_shapes=[
            pltpu.VMEM((levels, parts) + diag_inverse.shape[1:], f32),
            pltpu.VMEM((levels, local, 2, order, order), bf),
            pltpu.VMEM(off_diagonal.shape, bf),
            pltpu.VMEM((steps, local, order, off_diagonal.shape[2]), bf),
            pltpu.VMEM(right_sides.shape, f32),
            pltpu.VMEM(right_sides.shape, f32),
            pltpu.VMEM((outgoing * BR, cols), f32),
            pltpu.VMEM((local_rows * BR, cols), f32),
            pltpu.VMEM((steps, cut, n) + piece, bf),
            pltpu.VMEM((steps, cut, line) + piece, bf),
            pltpu.VMEM((steps, cut, line) + piece, bf),
            pltpu.VMEM((steps, cut, line) + piece, bf),
            [pltpu.VMEM((n * local_rows, BR, cols), bf)] * steps,
            pltpu.VMEM((outgoing * BR, cols), bf),
            dma((3, levels)),
            dma((levels, 2 * ymany)),
            dma((levels, 2 * ymany)),
            dma((steps, cut, line)),
            dma((steps, cut, line)),
            dma((steps, cut, line)),
            dma((steps, cut, line)),
            dma((steps, cut, line)),
            dma((steps, cut, line)),
            dma((steps, cut, line)),
            dma((steps, cut, line)),
            pltpu.SemaphoreType.REGULAR,
        ],
        compiler_params=pltpu.CompilerParams(
            collective_id=0, has_side_effects=True, vmem_limit_bytes=56 * 1024 * 1024
        ),
    )(right_sides, diag_inverse, off_diagonal, target_snode, target_block, target_snode,
      target_block)


def program(right_sides, diag_inverse, off_diagonal, target_snode, target_block):
    n, parts = lax.axis_size("snode"), lax.axis_size("rhs")
    capacity = 2 * right_sides.shape[1] * target_snode.shape[2] // n
    local_rows = right_sides.shape[1] * right_sides.shape[2] // BR
    dense = (
        capacity >= local_rows
        and n % PAIR == 0
        and parts % PAIR == 0
        and BR % right_sides.shape[1] == 0
    )
    body = dense_on_device if dense else on_device
    return body(right_sides, diag_inverse, off_diagonal, target_snode, target_block)


def solution(mesh):
    in_specs = (
        P(None, "snode", None, "rhs"),
        P(None, "snode", "rhs", None),
        P(None, "snode", None, None),
        P(None, "snode", None),
        P(None, "snode", None),
    )
    out_specs = P(None, "snode", None, "rhs")
    return jax.shard_map(
        program, mesh=mesh, in_specs=in_specs, out_specs=out_specs, check_vma=False
    )
```

```python
import functools

import jax
import jax.numpy as jnp
from jax import lax
from jax.experimental import pallas as pl
from jax.experimental.pallas import tpu as pltpu
from jax.sharding import PartitionSpec as P

BR = 16


def on_device(right_sides, diag_inverse, off_diagonal, target_snode, target_block):
    precise = lax.Precision.HIGHEST
    levels = right_sides.shape[0]
    local_nodes = right_sides.shape[1]
    order_size = right_sides.shape[2]
    columns = right_sides.shape[3]
    per_node = target_snode.shape[2]
    row_blocks = order_size // BR
    devices = lax.axis_size("snode")
    outgoing = local_nodes * per_node
    capacity = 2 * outgoing // devices
    slot_count = devices * capacity
    local_rows = local_nodes * row_blocks
    front_count = 1
    front_width = columns // front_count
    full_diag = [
        lax.all_gather(diag_inverse[height], "rhs", axis=1, tiled=True) for height in range(levels)
    ]
    block_order = lax.iota(jnp.int32, outgoing)
    slot_ids = lax.iota(jnp.int32, slot_count)
    row_ids = lax.iota(jnp.int32, local_rows)
    routes = []
    for height in range(levels - 1):
        flat_target = target_snode[height].reshape(outgoing)
        owner_dev = flat_target // local_nodes
        target_code = flat_target % local_nodes * row_blocks + target_block[height].reshape(
            outgoing
        )
        earlier = (owner_dev[:, None] == owner_dev[None, :]) & (
            block_order[None, :] < block_order[:, None]
        )
        destination = owner_dev * capacity + jnp.sum(earlier.astype(jnp.int32), axis=1)
        placed = destination[None, :] == slot_ids[:, None]
        source = jnp.max(jnp.where(placed, block_order[None, :], -1), axis=1)
        slot_code = jnp.max(jnp.where(placed, target_code[None, :], -1), axis=1).reshape(
            devices, capacity
        )
        routes.append((destination, source, slot_code))
    residual_list = [right_sides[0]]
    lower_sols = [[]]
    arrivals = [[]]
    for height in range(levels):
        front = 0
        solve_result = jnp.einsum(
            "svw,swr->svr", full_diag[height], residual_list[front], precision=precise
        )
        lower_sols[front].append(solve_result)
        if height + 1 < levels:
            destination, source, slot_code = routes[height]
            update = jnp.einsum(
                "skw,swr->skr",
                off_diagonal[height],
                solve_result.astype(jnp.bfloat16),
                preferred_element_type=jnp.float32,
            )
            update = update.astype(jnp.bfloat16).reshape(outgoing, BR * front_width)
            outbound = jnp.where(
                (source >= 0)[:, None], update[jnp.maximum(source, 0)], jnp.zeros((), jnp.bfloat16)
            )
            outbound = outbound.reshape(devices, capacity, BR * front_width)
            inbound, inbound_code = (
                lax.all_to_all(outbound, "snode", split_axis=0, concat_axis=0, tiled=True),
                lax.all_to_all(slot_code, "snode", split_axis=0, concat_axis=0, tiled=True),
            )
            arrived = inbound_code.reshape(slot_count)
            arrivals[front].append(arrived)
            gather_table = (arrived[None, :] == row_ids[:, None]).astype(jnp.bfloat16)
            summed = jnp.dot(
                gather_table,
                inbound.reshape(slot_count, BR * front_width),
                preferred_element_type=jnp.float32,
            )
            summed = summed.reshape(local_nodes, order_size, front_width)
            upcoming = right_sides[height + 1]
            residual_list[front] = upcoming - summed
    answer = [[None] * levels]
    for height in range(levels - 1, -1, -1):
        front = 0
        if height == levels - 1:
            carried = lower_sols[front][height]
        else:
            destination, source, slot_code = routes[height]
            above_rows = (
                answer[front][height + 1].astype(jnp.bfloat16).reshape(local_rows, BR * front_width)
            )
            arrived = arrivals[front][height]
            outbound = jnp.where(
                (arrived >= 0)[:, None],
                above_rows[jnp.maximum(arrived, 0)],
                jnp.zeros((), jnp.bfloat16),
            )
            outbound = outbound.reshape(devices, capacity, BR * front_width)
            returned = lax.all_to_all(outbound, "snode", split_axis=0, concat_axis=0, tiled=True)
            block_rows = returned.reshape(slot_count, BR * front_width)[destination]
            block_rows = block_rows.reshape(local_nodes, per_node * BR, front_width)
            carried = lower_sols[front][height] - jnp.einsum(
                "skw,skr->swr", off_diagonal[height], block_rows, preferred_element_type=jnp.float32
            )
        result = jnp.einsum("swv,swr->svr", full_diag[height], carried, precision=precise)
        answer[front][height] = result
    stacked = [answer[0][height] for height in range(levels)]
    return jnp.stack(stacked, axis=0)


MESH = pl.DeviceIdType.MESH
PAIR = 2


def mm(a, b):
    return jnp.dot(a, b, preferred_element_type=jnp.float32)


def split(a):
    high = a.astype(jnp.bfloat16)
    return high, (a - high.astype(jnp.float32)).astype(jnp.bfloat16)


def mm3(a_high, a_low, b):
    cols = b.shape[1]
    b_high, b_low = split(b)
    wide = mm(a_high, jnp.concatenate([b_high, b_low], axis=1))
    return wide[:, :cols] + wide[:, cols:] + mm(a_low, b_high)


def dense_kernel(
    n, parts, rs_hbm, dg_ref, od_hbm, snode_v, block_v, snode_s, block_s, out_ref,
    full, diag_t, od_ref, od_t, rs_ref, low, upd, nat, part, rx, rz, zs, above, picked,
    lsend, dsend, drecv, xsend, xrecv, zsend, zrecv, asend, arecv, bsend, brecv, token,
):
    levels, local, order, cols = rs_ref.shape
    per_node = snode_v.shape[2]
    outgoing = local * per_node
    row_blocks = order // BR
    local_rows = local * row_blocks
    line = n // PAIR
    ymany = parts // PAIR
    cut = local
    width = BR // cut
    me = lax.axis_index("snode")
    z, x = me // PAIR, me % PAIR
    mine = lax.axis_index("rhs")
    yy, cc = mine // PAIR, mine % PAIR
    mate = {"snode": z * PAIR + (1 - x)}
    bits = [1 << i for i in range(line.bit_length() - 1)]

    def flip(f):
        other = z
        for b in bits:
            if f & b:
                other = other + b - 2 * b * ((z // b) % 2)
        return other

    def lowest(f):
        return f & -f if f else line

    def feeders(f):
        return [f | b for b in bits if b < lowest(f)]

    peers = {b: {"snode": flip(b) * PAIR + x} for b in bits}
    inward = sorted(range(1, line), key=lambda f: (lowest(f), -f))
    outward = sorted(range(1, line), key=lambda f: (-lowest(f), f))
    twin = {"rhs": yy * PAIR + (1 - cc)}
    sides = [(yy + k) % ymany for k in range(1, ymany)]

    def remote(src, dst, s_sem, r_sem, where):
        return pltpu.make_async_remote_copy(
            src_ref=src, dst_ref=dst, send_sem=s_sem, recv_sem=r_sem,
            device_id=where, device_id_type=MESH,
        )

    barrier = pltpu.get_barrier_semaphore()

    def greet(where):
        pl.semaphore_signal(barrier, inc=1, device_id=where, device_id_type=MESH)

    greet(mate)
    greet(twin)
    for side in sides:
        greet({"rhs": side * PAIR + cc})

    for b in bits:
        greet(peers[b])

    own_diag = [
        pltpu.make_async_copy(dg_ref.at[h], full.at[h, mine], lsend.at[0, h])
        for h in range(levels)
    ]
    load_rs = [
        pltpu.make_async_copy(rs_hbm.at[h], rs_ref.at[h], lsend.at[1, h]) for h in range(levels)
    ]
    load_od = [
        pltpu.make_async_copy(od_hbm.at[h], od_ref.at[h], lsend.at[2, h])
        for h in range(levels - 1)
    ]
    for h in range(levels):
        own_diag[h].start()
        load_rs[h].start()
        if h < levels - 1:
            load_od[h].start()

    pl.semaphore_wait(barrier, ymany + 1 + len(bits))

    sent = []

    def start_gather(h):
        near = []
        for k, side in enumerate(sides):
            copy = remote(dg_ref.at[h], full.at[h, mine], dsend.at[h, k], drecv.at[h, k],
                          {"rhs": side * PAIR + cc})
            copy.start()
            near.append(copy)
        own = remote(dg_ref.at[h], full.at[h, mine], dsend.at[h, ymany], drecv.at[h, ymany], twin)
        own.start()
        return near, own

    def finish_gather(h, near, own, meanwhile=None):
        hops = []
        for k, copy in enumerate(near):
            copy.wait_recv()
            origin = ((yy + ymany - 1 - k) % ymany) * PAIR + cc
            hop = remote(full.at[h, origin], full.at[h, origin], dsend.at[h, ymany + 1 + k],
                         drecv.at[h, ymany + 1 + k], twin)
            hop.start()
            hops.append(hop)
        if meanwhile is not None:
            meanwhile()
        own.wait_recv()
        own_diag[h].wait()
        for hop in hops:
            hop.wait_recv()
        sent.extend(near + [own] + hops)

    def diag(h, s):
        return full[h, :, s].reshape(order, order)

    def forward(h, s, residual):
        high, low_part = split(diag(h, s))
        low[h, s] = mm3(high, low_part, residual)

    def backward(h, s, carried):
        out_ref[h, s] = mm3(diag_t[h, s, 0], diag_t[h, s, 1], carried)

    def prepare(h):
        for s in range(local):
            high, low_part = split(diag(h, s).T)
            diag_t[h, s, 0] = high
            diag_t[h, s, 1] = low_part

    def turn(h):
        for s in range(local):
            od_t[h, s] = od_ref[h, s].T

    def codes(h):
        code = snode_v[h] * row_blocks + block_v[h]
        return jnp.concatenate([code[s:s + 1] for s in range(local)], axis=1)

    def x_copy(h, q, k):
        return remote(part.at[h, q, flip(k) * PAIR + (1 - x)], rx.at[h, q, k], xsend.at[h, q, k],
                      xrecv.at[h, q, k], mate)

    def z_copy(h, q, k):
        return remote(zs.at[h, q, k], rz.at[h, q, k], zsend.at[h, q, k], zrecv.at[h, q, k],
                      peers[lowest(k)])

    first = start_gather(0)
    tables = []
    rows = lax.broadcasted_iota(jnp.int32, (n * local_rows, outgoing), 0)
    for h in range(levels - 1):
        tables.append(jnp.where(rows == codes(h), 1.0, 0.0).astype(jnp.bfloat16))
    load_od[0].wait()
    turn(0)

    def turn_rest():
        for h in range(1, levels - 1):
            load_od[h].wait()
            turn(h)

    finish_gather(0, *first, meanwhile=turn_rest)
    gather = [None] + [start_gather(h) for h in range(1, levels)]
    load_rs[0].wait()
    for s in range(local):
        forward(0, s, rs_ref[0, s])

    for h in range(levels - 1):
        for s in range(local):
            upd[pl.ds(s * per_node * BR, per_node * BR), :] = mm(
                od_ref[h, s], low[h, s].astype(jnp.bfloat16)
            )
        for q in range(cut):
            for r in range(width):
                piece = upd[pl.ds(q * width + r, outgoing, stride=BR), :].astype(jnp.bfloat16)
                summed = mm(tables[h], piece).astype(jnp.bfloat16)
                for d in range(n):
                    part[h, q, d, r * local_rows:(r + 1) * local_rows, :] = (
                        summed[d * local_rows:(d + 1) * local_rows]
                    )

            if h == 0 and q == 0:
                @pl.when(cc == 0)
                def _():
                    pl.semaphore_wait(token, 1)

            for k in inward + [0]:
                x_copy(h, q, k).start()

        def paired(q, k):
            x_copy(h, q, k).wait_recv()
            own = part[h, q, flip(k) * PAIR + x]
            total = own.astype(jnp.float32) + rx[h, q, k].astype(jnp.float32)
            for f in feeders(k):
                z_copy(h, q, f).wait_recv()
                total = total + rz[h, q, f].astype(jnp.float32)
            return total

        for q in range(cut):
            for k in inward:
                zs[h, q, k] = paired(q, k).astype(jnp.bfloat16)
                z_copy(h, q, k).start()
        if h == 0:
            for q in range(cut):
                for k in range(line):
                    x_copy(h, q, k).wait_send()

            @pl.when(cc == 1)
            def _():
                pl.semaphore_signal(token, inc=1, device_id=twin, device_id_type=MESH)

        prepare(h)
        finish_gather(h + 1, *gather[h + 1])
        if h == levels - 2:
            prepare(levels - 1)
        for q in range(cut):
            total = paired(q, 0)
            for r in range(width):
                nat[pl.ds(q * width + r, local_rows, stride=BR), :] = (
                    total[r * local_rows:(r + 1) * local_rows]
                )
        load_rs[h + 1].wait()
        for s in range(local):
            forward(h + 1, s, rs_ref[h + 1, s] - nat[pl.ds(s * order, order), :])

    def hop(h, q, source, where, s_sem, r_sem, col):
        slot = above[h].at[
            pl.ds(((source * PAIR + col) * local + q) * row_blocks, row_blocks)
        ]
        return remote(slot, slot, s_sem, r_sem, where)

    def line_hop(h, q, k, source):
        return hop(h, q, source, peers[lowest(k)], asend.at[h, q, k], arecv.at[h, q, k], x)

    def mate_hop(h, q, k, col):
        return hop(h, q, flip(k), mate, bsend.at[h, q, k], brecv.at[h, q, k], col)

    def publish(h, q):
        above[h][pl.ds((me * local + q) * row_blocks, row_blocks)] = (
            out_ref[h + 1, q].reshape(row_blocks, BR, cols).astype(jnp.bfloat16)
        )
        mate_hop(h, q, 0, x).start()
        for b in reversed(bits):
            line_hop(h, q, b, z).start()

    for s in range(local):
        backward(levels - 1, s, low[levels - 1, s])
        publish(levels - 2, s)

    for h in range(levels - 2, -1, -1):
        for k in outward:
            for q in range(cut):
                line_hop(h, q, k, flip(k)).wait_recv()
                for f in feeders(k):
                    line_hop(h, q, f, flip(k)).start()
                mate_hop(h, q, k, x).start()
        for q in range(cut):
            for k in range(line):
                mate_hop(h, q, k, 1 - x).wait_recv()
        for s in range(local):
            for k in range(per_node):
                picked[pl.ds((s * per_node + k) * BR, BR), :] = above[h][
                    snode_s[h, s, k] * row_blocks + block_s[h, s, k]
                ]
            carried = low[h, s] - mm(
                od_t[h, s], picked[pl.ds(s * per_node * BR, per_node * BR), :]
            )
            backward(h, s, carried)
            if h > 0:
                publish(h - 1, s)

    for copy in sent:
        copy.wait_send()
    for h in range(levels - 1):
        for q in range(cut):
            for k in range(line):
                if h > 0:
                    x_copy(h, q, k).wait_send()
                mate_hop(h, q, k, x).wait_send()
            for k in inward:
                z_copy(h, q, k).wait_send()
                line_hop(h, q, k, z).wait_send()


def dense_on_device(right_sides, diag_inverse, off_diagonal, target_snode, target_block):
    levels, local, order, cols = right_sides.shape
    n, parts = lax.axis_size("snode"), lax.axis_size("rhs")
    outgoing = local * target_snode.shape[2]
    row_blocks = order // BR
    local_rows = local * row_blocks
    line = n // PAIR
    ymany = parts // PAIR
    cut = local
    piece = (local_rows * BR // cut, cols)
    bf, f32 = jnp.bfloat16, jnp.float32
    steps = levels - 1
    dma = pltpu.SemaphoreType.DMA
    vmem = pl.BlockSpec(memory_space=pltpu.VMEM)
    smem = pl.BlockSpec(memory_space=pltpu.SMEM)
    hbm = pl.BlockSpec(memory_space=pltpu.HBM)
    return pl.pallas_call(
        functools.partial(dense_kernel, n, parts),
        out_shape=jax.ShapeDtypeStruct(right_sides.shape, f32),
        in_specs=[hbm] * 3 + [vmem] * 2 + [smem] * 2,
        out_specs=vmem,
        scratch_shapes=[
            pltpu.VMEM((levels, parts) + diag_inverse.shape[1:], f32),
            pltpu.VMEM((levels, local, 2, order, order), bf),
            pltpu.VMEM(off_diagonal.shape, bf),
            pltpu.VMEM((steps, local, order, off_diagonal.shape[2]), bf),
            pltpu.VMEM(right_sides.shape, f32),
            pltpu.VMEM(right_sides.shape, f32),
            pltpu.VMEM((outgoing * BR, cols), f32),
            pltpu.VMEM((local_rows * BR, cols), f32),
            pltpu.VMEM((steps, cut, n) + piece, bf),
            pltpu.VMEM((steps, cut, line) + piece, bf),
            pltpu.VMEM((steps, cut, line) + piece, bf),
            pltpu.VMEM((steps, cut, line) + piece, bf),
            [pltpu.VMEM((n * local_rows, BR, cols), bf)] * steps,
            pltpu.VMEM((outgoing * BR, cols), bf),
            dma((3, levels)),
            dma((levels, 2 * ymany)),
            dma((levels, 2 * ymany)),
            dma((steps, cut, line)),
            dma((steps, cut, line)),
            dma((steps, cut, line)),
            dma((steps, cut, line)),
            dma((steps, cut, line)),
            dma((steps, cut, line)),
            dma((steps, cut, line)),
            dma((steps, cut, line)),
            pltpu.SemaphoreType.REGULAR,
        ],
        compiler_params=pltpu.CompilerParams(
            collective_id=0, has_side_effects=True, vmem_limit_bytes=56 * 1024 * 1024
        ),
    )(right_sides, diag_inverse, off_diagonal, target_snode, target_block, target_snode,
      target_block)


def program(right_sides, diag_inverse, off_diagonal, target_snode, target_block):
    n, parts = lax.axis_size("snode"), lax.axis_size("rhs")
    capacity = 2 * right_sides.shape[1] * target_snode.shape[2] // n
    local_rows = right_sides.shape[1] * right_sides.shape[2] // BR
    dense = (
        capacity >= local_rows
        and n % PAIR == 0
        and (n // PAIR) & (n // PAIR - 1) == 0
        and parts % PAIR == 0
        and BR % right_sides.shape[1] == 0
    )
    body = dense_on_device if dense else on_device
    return body(right_sides, diag_inverse, off_diagonal, target_snode, target_block)


def solution(mesh):
    in_specs = (
        P(None, "snode", None, "rhs"),
        P(None, "snode", "rhs", None),
        P(None, "snode", None, None),
        P(None, "snode", None),
        P(None, "snode", None),
    )
    out_specs = P(None, "snode", None, "rhs")
    return jax.shard_map(
        program, mesh=mesh, in_specs=in_specs, out_specs=out_specs, check_vma=False
    )
```

```python
import functools

import jax
import jax.numpy as jnp
from jax import lax
from jax.experimental import pallas as pl
from jax.experimental.pallas import tpu as pltpu
from jax.sharding import PartitionSpec as P

BR = 16


def on_device(right_sides, diag_inverse, off_diagonal, target_snode, target_block):
    precise = lax.Precision.HIGHEST
    levels = right_sides.shape[0]
    local_nodes = right_sides.shape[1]
    order_size = right_sides.shape[2]
    columns = right_sides.shape[3]
    per_node = target_snode.shape[2]
    row_blocks = order_size // BR
    devices = lax.axis_size("snode")
    outgoing = local_nodes * per_node
    capacity = 2 * outgoing // devices
    slot_count = devices * capacity
    local_rows = local_nodes * row_blocks
    front_count = 1
    front_width = columns // front_count
    full_diag = [
        lax.all_gather(diag_inverse[height], "rhs", axis=1, tiled=True) for height in range(levels)
    ]
    block_order = lax.iota(jnp.int32, outgoing)
    slot_ids = lax.iota(jnp.int32, slot_count)
    row_ids = lax.iota(jnp.int32, local_rows)
    routes = []
    for height in range(levels - 1):
        flat_target = target_snode[height].reshape(outgoing)
        owner_dev = flat_target // local_nodes
        target_code = flat_target % local_nodes * row_blocks + target_block[height].reshape(
            outgoing
        )
        earlier = (owner_dev[:, None] == owner_dev[None, :]) & (
            block_order[None, :] < block_order[:, None]
        )
        destination = owner_dev * capacity + jnp.sum(earlier.astype(jnp.int32), axis=1)
        placed = destination[None, :] == slot_ids[:, None]
        source = jnp.max(jnp.where(placed, block_order[None, :], -1), axis=1)
        slot_code = jnp.max(jnp.where(placed, target_code[None, :], -1), axis=1).reshape(
            devices, capacity
        )
        routes.append((destination, source, slot_code))
    residual_list = [right_sides[0]]
    lower_sols = [[]]
    arrivals = [[]]
    for height in range(levels):
        front = 0
        solve_result = jnp.einsum(
            "svw,swr->svr", full_diag[height], residual_list[front], precision=precise
        )
        lower_sols[front].append(solve_result)
        if height + 1 < levels:
            destination, source, slot_code = routes[height]
            update = jnp.einsum(
                "skw,swr->skr",
                off_diagonal[height],
                solve_result.astype(jnp.bfloat16),
                preferred_element_type=jnp.float32,
            )
            update = update.astype(jnp.bfloat16).reshape(outgoing, BR * front_width)
            outbound = jnp.where(
                (source >= 0)[:, None], update[jnp.maximum(source, 0)], jnp.zeros((), jnp.bfloat16)
            )
            outbound = outbound.reshape(devices, capacity, BR * front_width)
            inbound, inbound_code = (
                lax.all_to_all(outbound, "snode", split_axis=0, concat_axis=0, tiled=True),
                lax.all_to_all(slot_code, "snode", split_axis=0, concat_axis=0, tiled=True),
            )
            arrived = inbound_code.reshape(slot_count)
            arrivals[front].append(arrived)
            gather_table = (arrived[None, :] == row_ids[:, None]).astype(jnp.bfloat16)
            summed = jnp.dot(
                gather_table,
                inbound.reshape(slot_count, BR * front_width),
                preferred_element_type=jnp.float32,
            )
            summed = summed.reshape(local_nodes, order_size, front_width)
            upcoming = right_sides[height + 1]
            residual_list[front] = upcoming - summed
    answer = [[None] * levels]
    for height in range(levels - 1, -1, -1):
        front = 0
        if height == levels - 1:
            carried = lower_sols[front][height]
        else:
            destination, source, slot_code = routes[height]
            above_rows = (
                answer[front][height + 1].astype(jnp.bfloat16).reshape(local_rows, BR * front_width)
            )
            arrived = arrivals[front][height]
            outbound = jnp.where(
                (arrived >= 0)[:, None],
                above_rows[jnp.maximum(arrived, 0)],
                jnp.zeros((), jnp.bfloat16),
            )
            outbound = outbound.reshape(devices, capacity, BR * front_width)
            returned = lax.all_to_all(outbound, "snode", split_axis=0, concat_axis=0, tiled=True)
            block_rows = returned.reshape(slot_count, BR * front_width)[destination]
            block_rows = block_rows.reshape(local_nodes, per_node * BR, front_width)
            carried = lower_sols[front][height] - jnp.einsum(
                "skw,skr->swr", off_diagonal[height], block_rows, preferred_element_type=jnp.float32
            )
        result = jnp.einsum("swv,swr->svr", full_diag[height], carried, precision=precise)
        answer[front][height] = result
    stacked = [answer[0][height] for height in range(levels)]
    return jnp.stack(stacked, axis=0)


MESH = pl.DeviceIdType.MESH
PAIR = 2


def mm(a, b):
    return jnp.dot(a, b, preferred_element_type=jnp.float32)


def split(a):
    high = a.astype(jnp.bfloat16)
    return high, (a - high.astype(jnp.float32)).astype(jnp.bfloat16)


def mm3(a_high, a_low, b):
    cols = b.shape[1]
    b_high, b_low = split(b)
    wide = mm(a_high, jnp.concatenate([b_high, b_low], axis=1))
    return wide[:, :cols] + wide[:, cols:] + mm(a_low, b_high)


def dense_kernel(
    n, parts, rs_hbm, dg_ref, od_hbm, snode_v, block_v, snode_s, block_s, outs,
    full, diag_t, od_ref, od_t, rs_ref, low, upd, nat, part, rx, rz, zs, above, picked,
    lsend, dsend, drecv, xsend, xrecv, zsend, zrecv, asend, arecv, bsend, brecv, token,
):
    levels, local, order, cols = rs_ref.shape
    per_node = snode_v.shape[2]
    outgoing = local * per_node
    row_blocks = order // BR
    local_rows = local * row_blocks
    line = n // PAIR
    ymany = parts // PAIR
    cut = local
    width = BR // cut
    me = lax.axis_index("snode")
    z, x = me // PAIR, me % PAIR
    mine = lax.axis_index("rhs")
    yy, cc = mine // PAIR, mine % PAIR
    mate = {"snode": z * PAIR + (1 - x)}
    away = [k for k in (2, 1) if k < line] + list(range(3, line))
    peers = {k: {"snode": (z + k) % line * PAIR + x} for k in away}
    twin = {"rhs": yy * PAIR + (1 - cc)}
    sides = [(yy + k) % ymany for k in range(1, ymany)]

    def remote(src, dst, s_sem, r_sem, where):
        return pltpu.make_async_remote_copy(
            src_ref=src, dst_ref=dst, send_sem=s_sem, recv_sem=r_sem,
            device_id=where, device_id_type=MESH,
        )

    barrier = pltpu.get_barrier_semaphore()

    def greet(where):
        pl.semaphore_signal(barrier, inc=1, device_id=where, device_id_type=MESH)

    greet(mate)
    greet(twin)
    for side in sides:
        greet({"rhs": side * PAIR + cc})

    for k in away:
        greet(peers[k])

    own_diag = [
        pltpu.make_async_copy(dg_ref.at[h], full.at[h, mine], lsend.at[0, h])
        for h in range(levels)
    ]
    load_rs = [
        pltpu.make_async_copy(rs_hbm.at[h], rs_ref.at[h], lsend.at[1, h]) for h in range(levels)
    ]
    load_od = [
        pltpu.make_async_copy(od_hbm.at[h], od_ref.at[h], lsend.at[2, h])
        for h in range(levels - 1)
    ]
    for h in range(levels):
        own_diag[h].start()
        load_rs[h].start()
        if h < levels - 1:
            load_od[h].start()

    pl.semaphore_wait(barrier, ymany + line)

    sent = []

    def start_gather(h):
        near = []
        for k, side in enumerate(sides):
            copy = remote(dg_ref.at[h], full.at[h, mine], dsend.at[h, k], drecv.at[h, k],
                          {"rhs": side * PAIR + cc})
            copy.start()
            near.append(copy)
        own = remote(dg_ref.at[h], full.at[h, mine], dsend.at[h, ymany], drecv.at[h, ymany], twin)
        own.start()
        return near, own

    def finish_gather(h, near, own, meanwhile=None):
        hops = []
        for k, copy in enumerate(near):
            copy.wait_recv()
            origin = ((yy + ymany - 1 - k) % ymany) * PAIR + cc
            hop = remote(full.at[h, origin], full.at[h, origin], dsend.at[h, ymany + 1 + k],
                         drecv.at[h, ymany + 1 + k], twin)
            hop.start()
            hops.append(hop)
        if meanwhile is not None:
            meanwhile()
        own.wait_recv()
        own_diag[h].wait()
        for hop in hops:
            hop.wait_recv()
        sent.extend(near + [own] + hops)

    def diag(h, s):
        return full[h, :, s].reshape(order, order)

    def forward(h, s, residual):
        high, low_part = split(diag(h, s))
        low[h, s] = mm3(high, low_part, residual)

    def backward(h, s, carried):
        outs[h][s] = mm3(diag_t[h, s, 0], diag_t[h, s, 1], carried)

    def prepare(h):
        for s in range(local):
            high, low_part = split(diag(h, s).T)
            diag_t[h, s, 0] = high
            diag_t[h, s, 1] = low_part

    def turn(h):
        for s in range(local):
            od_t[h, s] = od_ref[h, s].T

    def codes(h):
        code = snode_v[h] * row_blocks + block_v[h]
        return jnp.concatenate([code[s:s + 1] for s in range(local)], axis=1)

    def x_copy(h, q, k):
        d = (z + k) % line
        return remote(part.at[h, q, d * PAIR + (1 - x)], rx.at[h, q, k], xsend.at[h, q, k],
                      xrecv.at[h, q, k], mate)

    def z_copy(h, q, k):
        return remote(zs.at[h, q, k], rz.at[h, q, k], zsend.at[h, q, k], zrecv.at[h, q, k], peers[k])

    first = start_gather(0)
    tables = []
    rows = lax.broadcasted_iota(jnp.int32, (n * local_rows, outgoing), 0)
    for h in range(levels - 1):
        tables.append(jnp.where(rows == codes(h), 1.0, 0.0).astype(jnp.bfloat16))
    load_od[0].wait()
    turn(0)

    def turn_rest():
        for h in range(1, levels - 1):
            load_od[h].wait()
            turn(h)

    finish_gather(0, *first, meanwhile=turn_rest)
    gather = [None] + [start_gather(h) for h in range(1, levels)]
    load_rs[0].wait()
    for s in range(local):
        forward(0, s, rs_ref[0, s])

    for h in range(levels - 1):
        for s in range(local):
            upd[pl.ds(s * per_node * BR, per_node * BR), :] = mm(
                od_ref[h, s], low[h, s].astype(jnp.bfloat16)
            )
        for q in range(cut):
            for r in range(width):
                piece = upd[pl.ds(q * width + r, outgoing, stride=BR), :].astype(jnp.bfloat16)
                summed = mm(tables[h], piece).astype(jnp.bfloat16)
                for d in range(n):
                    part[h, q, d, r * local_rows:(r + 1) * local_rows, :] = (
                        summed[d * local_rows:(d + 1) * local_rows]
                    )

            if h == 0 and q == 0:
                @pl.when(cc == 0)
                def _():
                    pl.semaphore_wait(token, 1)

            for k in away + [0]:
                x_copy(h, q, k).start()

        def paired(q, k):
            x_copy(h, q, k).wait_recv()
            own = part[h, q, (z + k) % line * PAIR + x]
            return own.astype(jnp.float32) + rx[h, q, k].astype(jnp.float32)

        for q in range(cut):
            for k in away:
                zs[h, q, k] = paired(q, k).astype(jnp.bfloat16)
                z_copy(h, q, k).start()
        if h == 0:
            for q in range(cut):
                for k in range(line):
                    x_copy(h, q, k).wait_send()

            @pl.when(cc == 1)
            def _():
                pl.semaphore_signal(token, inc=1, device_id=twin, device_id_type=MESH)

        if h == 0:
            prepare(0)
        finish_gather(h + 1, *gather[h + 1])
        if h == levels - 2:
            prepare(levels - 1)
        for q in range(cut):
            total = paired(q, 0)
            for k in away:
                z_copy(h, q, k).wait_recv()
                total = total + rz[h, q, k].astype(jnp.float32)
            for r in range(width):
                nat[pl.ds(q * width + r, local_rows, stride=BR), :] = (
                    total[r * local_rows:(r + 1) * local_rows]
                )
        load_rs[h + 1].wait()
        for s in range(local):
            forward(h + 1, s, rs_ref[h + 1, s] - nat[pl.ds(s * order, order), :])

    def hop(h, q, source, where, s_sem, r_sem, col):
        slot = above[h].at[
            pl.ds(((source * PAIR + col) * local + q) * row_blocks, row_blocks)
        ]
        return remote(slot, slot, s_sem, r_sem, where)

    def line_hop(h, q, k, source):
        return hop(h, q, source, peers[k], asend.at[h, q, k], arecv.at[h, q, k], x)

    def mate_hop(h, q, k, col):
        source = (z + line - k) % line
        return hop(h, q, source, mate, bsend.at[h, q, k], brecv.at[h, q, k], col)

    def publish(h, q):
        above[h][pl.ds((me * local + q) * row_blocks, row_blocks)] = (
            outs[h + 1][q].reshape(row_blocks, BR, cols).astype(jnp.bfloat16)
        )
        mate_hop(h, q, 0, x).start()
        for k in away:
            line_hop(h, q, k, z).start()

    for s in range(local):
        backward(levels - 1, s, low[levels - 1, s])
        publish(levels - 2, s)

    for h in range(levels - 2, -1, -1):
        if h > 0:
            prepare(h)
        for q in range(cut):
            for k in away:
                line_hop(h, q, k, (z + line - k) % line).wait_recv()
                mate_hop(h, q, k, x).start()
        for q in range(cut):
            for k in range(line):
                mate_hop(h, q, k, 1 - x).wait_recv()
        for s in range(local):
            for k in range(per_node):
                picked[pl.ds((s * per_node + k) * BR, BR), :] = above[h][
                    snode_s[h, s, k] * row_blocks + block_s[h, s, k]
                ]
            carried = low[h, s] - mm(
                od_t[h, s], picked[pl.ds(s * per_node * BR, per_node * BR), :]
            )
            backward(h, s, carried)
            if h > 0:
                publish(h - 1, s)

    for copy in sent:
        copy.wait_send()
    for h in range(levels - 1):
        for q in range(cut):
            for k in range(line):
                if h > 0:
                    x_copy(h, q, k).wait_send()
                mate_hop(h, q, k, x).wait_send()
            for k in away:
                z_copy(h, q, k).wait_send()
                line_hop(h, q, k, z).wait_send()


def dense_on_device(right_sides, diag_inverse, off_diagonal, target_snode, target_block):
    levels, local, order, cols = right_sides.shape
    n, parts = lax.axis_size("snode"), lax.axis_size("rhs")
    outgoing = local * target_snode.shape[2]
    row_blocks = order // BR
    local_rows = local * row_blocks
    line = n // PAIR
    ymany = parts // PAIR
    cut = local
    piece = (local_rows * BR // cut, cols)
    bf, f32 = jnp.bfloat16, jnp.float32
    steps = levels - 1
    dma = pltpu.SemaphoreType.DMA
    vmem = pl.BlockSpec(memory_space=pltpu.VMEM)
    smem = pl.BlockSpec(memory_space=pltpu.SMEM)
    hbm = pl.BlockSpec(memory_space=pltpu.HBM)
    answers = pl.pallas_call(
        functools.partial(dense_kernel, n, parts),
        out_shape=[[jax.ShapeDtypeStruct(right_sides.shape[1:], f32)] * levels],
        in_specs=[hbm] * 3 + [vmem] * 2 + [smem] * 2,
        out_specs=[[vmem] * levels],
        scratch_shapes=[
            pltpu.VMEM((levels, parts) + diag_inverse.shape[1:], f32),
            pltpu.VMEM((levels, local, 2, order, order), bf),
            pltpu.VMEM(off_diagonal.shape, bf),
            pltpu.VMEM((steps, local, order, off_diagonal.shape[2]), bf),
            pltpu.VMEM(right_sides.shape, f32),
            pltpu.VMEM(right_sides.shape, f32),
            pltpu.VMEM((outgoing * BR, cols), f32),
            pltpu.VMEM((local_rows * BR, cols), f32),
            pltpu.VMEM((steps, cut, n) + piece, bf),
            pltpu.VMEM((steps, cut, line) + piece, bf),
            pltpu.VMEM((steps, cut, line) + piece, bf),
            pltpu.VMEM((steps, cut, line) + piece, bf),
            [pltpu.VMEM((n * local_rows, BR, cols), bf)] * steps,
            pltpu.VMEM((outgoing * BR, cols), bf),
            dma((3, levels)),
            dma((levels, 2 * ymany)),
            dma((levels, 2 * ymany)),
            dma((steps, cut, line)),
            dma((steps, cut, line)),
            dma((steps, cut, line)),
            dma((steps, cut, line)),
            dma((steps, cut, line)),
            dma((steps, cut, line)),
            dma((steps, cut, line)),
            dma((steps, cut, line)),
            pltpu.SemaphoreType.REGULAR,
        ],
        compiler_params=pltpu.CompilerParams(
            collective_id=0, has_side_effects=True, vmem_limit_bytes=56 * 1024 * 1024
        ),
    )(right_sides, diag_inverse, off_diagonal, target_snode, target_block, target_snode,
      target_block)
    return jnp.stack(answers[0], axis=0)


def program(right_sides, diag_inverse, off_diagonal, target_snode, target_block):
    n, parts = lax.axis_size("snode"), lax.axis_size("rhs")
    capacity = 2 * right_sides.shape[1] * target_snode.shape[2] // n
    local_rows = right_sides.shape[1] * right_sides.shape[2] // BR
    dense = (
        capacity >= local_rows
        and n % PAIR == 0
        and parts % PAIR == 0
        and BR % right_sides.shape[1] == 0
    )
    body = dense_on_device if dense else on_device
    return body(right_sides, diag_inverse, off_diagonal, target_snode, target_block)


def solution(mesh):
    in_specs = (
        P(None, "snode", None, "rhs"),
        P(None, "snode", "rhs", None),
        P(None, "snode", None, None),
        P(None, "snode", None),
        P(None, "snode", None),
    )
    out_specs = P(None, "snode", None, "rhs")
    return jax.shard_map(
        program, mesh=mesh, in_specs=in_specs, out_specs=out_specs, check_vma=False
    )
```

```python
import functools

import jax
import jax.numpy as jnp
from jax import lax
from jax.experimental import pallas as pl
from jax.experimental.pallas import tpu as pltpu
from jax.sharding import PartitionSpec as P

BR = 16


def on_device(right_sides, diag_inverse, off_diagonal, target_snode, target_block):
    precise = lax.Precision.HIGHEST
    levels = right_sides.shape[0]
    local_nodes = right_sides.shape[1]
    order_size = right_sides.shape[2]
    columns = right_sides.shape[3]
    per_node = target_snode.shape[2]
    row_blocks = order_size // BR
    devices = lax.axis_size("snode")
    outgoing = local_nodes * per_node
    capacity = 2 * outgoing // devices
    slot_count = devices * capacity
    local_rows = local_nodes * row_blocks
    front_count = 1
    front_width = columns // front_count
    full_diag = [
        lax.all_gather(diag_inverse[height], "rhs", axis=1, tiled=True) for height in range(levels)
    ]
    block_order = lax.iota(jnp.int32, outgoing)
    slot_ids = lax.iota(jnp.int32, slot_count)
    row_ids = lax.iota(jnp.int32, local_rows)
    routes = []
    for height in range(levels - 1):
        flat_target = target_snode[height].reshape(outgoing)
        owner_dev = flat_target // local_nodes
        target_code = flat_target % local_nodes * row_blocks + target_block[height].reshape(
            outgoing
        )
        earlier = (owner_dev[:, None] == owner_dev[None, :]) & (
            block_order[None, :] < block_order[:, None]
        )
        destination = owner_dev * capacity + jnp.sum(earlier.astype(jnp.int32), axis=1)
        placed = destination[None, :] == slot_ids[:, None]
        source = jnp.max(jnp.where(placed, block_order[None, :], -1), axis=1)
        slot_code = jnp.max(jnp.where(placed, target_code[None, :], -1), axis=1).reshape(
            devices, capacity
        )
        routes.append((destination, source, slot_code))
    residual_list = [right_sides[0]]
    lower_sols = [[]]
    arrivals = [[]]
    for height in range(levels):
        front = 0
        solve_result = jnp.einsum(
            "svw,swr->svr", full_diag[height], residual_list[front], precision=precise
        )
        lower_sols[front].append(solve_result)
        if height + 1 < levels:
            destination, source, slot_code = routes[height]
            update = jnp.einsum(
                "skw,swr->skr",
                off_diagonal[height],
                solve_result.astype(jnp.bfloat16),
                preferred_element_type=jnp.float32,
            )
            update = update.astype(jnp.bfloat16).reshape(outgoing, BR * front_width)
            outbound = jnp.where(
                (source >= 0)[:, None], update[jnp.maximum(source, 0)], jnp.zeros((), jnp.bfloat16)
            )
            outbound = outbound.reshape(devices, capacity, BR * front_width)
            inbound, inbound_code = (
                lax.all_to_all(outbound, "snode", split_axis=0, concat_axis=0, tiled=True),
                lax.all_to_all(slot_code, "snode", split_axis=0, concat_axis=0, tiled=True),
            )
            arrived = inbound_code.reshape(slot_count)
            arrivals[front].append(arrived)
            gather_table = (arrived[None, :] == row_ids[:, None]).astype(jnp.bfloat16)
            summed = jnp.dot(
                gather_table,
                inbound.reshape(slot_count, BR * front_width),
                preferred_element_type=jnp.float32,
            )
            summed = summed.reshape(local_nodes, order_size, front_width)
            upcoming = right_sides[height + 1]
            residual_list[front] = upcoming - summed
    answer = [[None] * levels]
    for height in range(levels - 1, -1, -1):
        front = 0
        if height == levels - 1:
            carried = lower_sols[front][height]
        else:
            destination, source, slot_code = routes[height]
            above_rows = (
                answer[front][height + 1].astype(jnp.bfloat16).reshape(local_rows, BR * front_width)
            )
            arrived = arrivals[front][height]
            outbound = jnp.where(
                (arrived >= 0)[:, None],
                above_rows[jnp.maximum(arrived, 0)],
                jnp.zeros((), jnp.bfloat16),
            )
            outbound = outbound.reshape(devices, capacity, BR * front_width)
            returned = lax.all_to_all(outbound, "snode", split_axis=0, concat_axis=0, tiled=True)
            block_rows = returned.reshape(slot_count, BR * front_width)[destination]
            block_rows = block_rows.reshape(local_nodes, per_node * BR, front_width)
            carried = lower_sols[front][height] - jnp.einsum(
                "skw,skr->swr", off_diagonal[height], block_rows, preferred_element_type=jnp.float32
            )
        result = jnp.einsum("swv,swr->svr", full_diag[height], carried, precision=precise)
        answer[front][height] = result
    stacked = [answer[0][height] for height in range(levels)]
    return jnp.stack(stacked, axis=0)


MESH = pl.DeviceIdType.MESH
PAIR = 2


def mm(a, b):
    return jnp.dot(a, b, preferred_element_type=jnp.float32)


def split(a):
    high = a.astype(jnp.bfloat16)
    return high, (a - high.astype(jnp.float32)).astype(jnp.bfloat16)


def mm3(a_high, a_low, b):
    cols = b.shape[1]
    b_high, b_low = split(b)
    wide = mm(a_high, jnp.concatenate([b_high, b_low], axis=1))
    return wide[:, :cols] + wide[:, cols:] + mm(a_low, b_high)


def dense_kernel(
    n, parts, rs_hbm, dg_ref, od_hbm, snode_v, block_v, snode_s, block_s, outs,
    full, diag_t, od_ref, od_t, rs_ref, low, upd, nat, part, rx, rz, zs, above, picked,
    lsend, dsend, drecv, xsend, xrecv, zsend, zrecv, asend, arecv, bsend, brecv, token,
):
    levels, local, order, cols = rs_ref.shape
    per_node = snode_v.shape[2]
    outgoing = local * per_node
    row_blocks = order // BR
    local_rows = local * row_blocks
    line = n // PAIR
    ymany = parts // PAIR
    cut = local
    width = BR // cut
    me = lax.axis_index("snode")
    z, x = me // PAIR, me % PAIR
    mine = lax.axis_index("rhs")
    yy, cc = mine // PAIR, mine % PAIR
    mate = {"snode": z * PAIR + (1 - x)}
    away = [k for k in (2, 1) if k < line] + list(range(3, line))
    peers = {k: {"snode": (z + k) % line * PAIR + x} for k in away}
    twin = {"rhs": yy * PAIR + (1 - cc)}
    sides = [(yy + k) % ymany for k in range(1, ymany)]

    def remote(src, dst, s_sem, r_sem, where):
        return pltpu.make_async_remote_copy(
            src_ref=src, dst_ref=dst, send_sem=s_sem, recv_sem=r_sem,
            device_id=where, device_id_type=MESH,
        )

    barrier = pltpu.get_barrier_semaphore()

    def greet(where):
        pl.semaphore_signal(barrier, inc=1, device_id=where, device_id_type=MESH)

    greet(mate)
    greet(twin)
    for side in sides:
        greet({"rhs": side * PAIR + cc})

    for k in away:
        greet(peers[k])

    own_diag = [
        pltpu.make_async_copy(dg_ref.at[h], full.at[h, mine], lsend.at[0, h])
        for h in range(levels)
    ]
    load_rs = [
        pltpu.make_async_copy(rs_hbm.at[h], rs_ref.at[h], lsend.at[1, h]) for h in range(levels)
    ]
    load_od = [
        pltpu.make_async_copy(od_hbm.at[h], od_ref.at[h], lsend.at[2, h])
        for h in range(levels - 1)
    ]
    for h in range(levels):
        own_diag[h].start()
        load_rs[h].start()
        if h < levels - 1:
            load_od[h].start()

    pl.semaphore_wait(barrier, ymany + line)

    sent = []

    def start_gather(h):
        near = []
        for k, side in enumerate(sides):
            copy = remote(dg_ref.at[h], full.at[h, mine], dsend.at[h, k], drecv.at[h, k],
                          {"rhs": side * PAIR + cc})
            copy.start()
            near.append(copy)
        own = remote(dg_ref.at[h], full.at[h, mine], dsend.at[h, ymany], drecv.at[h, ymany], twin)
        own.start()
        return near, own

    def finish_gather(h, near, own, meanwhile=None):
        hops = []
        for k, copy in enumerate(near):
            copy.wait_recv()
            origin = ((yy + ymany - 1 - k) % ymany) * PAIR + cc
            hop = remote(full.at[h, origin], full.at[h, origin], dsend.at[h, ymany + 1 + k],
                         drecv.at[h, ymany + 1 + k], twin)
            hop.start()
            hops.append(hop)
        if meanwhile is not None:
            meanwhile()
        own.wait_recv()
        own_diag[h].wait()
        for hop in hops:
            hop.wait_recv()
        sent.extend(near + [own] + hops)

    def diag(h, s):
        return full[h, :, s].reshape(order, order)

    def forward(h, s, residual):
        high, low_part = split(diag(h, s))
        low[h, s] = mm3(high, low_part, residual)

    def backward(h, s, carried):
        outs[h][s] = mm3(diag_t[h, s, 0], diag_t[h, s, 1], carried)

    def prepare(h):
        for s in range(local):
            high, low_part = split(diag(h, s).T)
            diag_t[h, s, 0] = high
            diag_t[h, s, 1] = low_part

    def turn(h):
        for s in range(local):
            od_t[h, s] = od_ref[h, s].T

    def codes(h):
        code = snode_v[h] * row_blocks + block_v[h]
        return jnp.concatenate([code[s:s + 1] for s in range(local)], axis=1)

    def x_copy(h, q, k):
        d = (z + k) % line
        return remote(part.at[h, q, d * PAIR + (1 - x)], rx.at[h, q, k], xsend.at[h, q, k],
                      xrecv.at[h, q, k], mate)

    def z_copy(h, q, k):
        return remote(zs.at[h, q, k], rz.at[h, q, k], zsend.at[h, q, k], zrecv.at[h, q, k], peers[k])

    last = [(cut - 1, away[-1]), (cut - 1, 0)]
    released = [(q, k) for q in range(cut) for k in away + [0] if (q, k) not in last]
    first = start_gather(0)
    tables = []
    rows = lax.broadcasted_iota(jnp.int32, (n * local_rows, outgoing), 0)
    for h in range(levels - 1):
        tables.append(jnp.where(rows == codes(h), 1.0, 0.0).astype(jnp.bfloat16))
    load_od[0].wait()
    turn(0)

    def turn_rest():
        for h in range(1, levels - 1):
            load_od[h].wait()
            turn(h)

    finish_gather(0, *first, meanwhile=turn_rest)
    gather = [None] + [start_gather(h) for h in range(1, levels)]
    load_rs[0].wait()
    for s in range(local):
        forward(0, s, rs_ref[0, s])

    for h in range(levels - 1):
        for s in range(local):
            upd[pl.ds(s * per_node * BR, per_node * BR), :] = mm(
                od_ref[h, s], low[h, s].astype(jnp.bfloat16)
            )
        for q in range(cut):
            for r in range(width):
                piece = upd[pl.ds(q * width + r, outgoing, stride=BR), :].astype(jnp.bfloat16)
                summed = mm(tables[h], piece).astype(jnp.bfloat16)
                for d in range(n):
                    part[h, q, d, r * local_rows:(r + 1) * local_rows, :] = (
                        summed[d * local_rows:(d + 1) * local_rows]
                    )

            if h == 0 and q == 0:
                @pl.when(cc == 0)
                def _():
                    pl.semaphore_wait(token, 1)

            for k in away + [0]:
                x_copy(h, q, k).start()

        def paired(q, k):
            x_copy(h, q, k).wait_recv()
            own = part[h, q, (z + k) % line * PAIR + x]
            return own.astype(jnp.float32) + rx[h, q, k].astype(jnp.float32)

        for q in range(cut):
            for k in away:
                if h == 0 and (q, k) == (cut - 1, away[-1]):
                    for early in released:
                        x_copy(h, *early).wait_send()

                    @pl.when(cc == 1)
                    def _():
                        pl.semaphore_signal(token, inc=1, device_id=twin, device_id_type=MESH)

                zs[h, q, k] = paired(q, k).astype(jnp.bfloat16)
                z_copy(h, q, k).start()
        if h == 0:
            prepare(0)
        finish_gather(h + 1, *gather[h + 1])
        if h == levels - 2:
            prepare(levels - 1)
        for q in range(cut):
            total = paired(q, 0)
            for k in away:
                z_copy(h, q, k).wait_recv()
                total = total + rz[h, q, k].astype(jnp.float32)
            for r in range(width):
                nat[pl.ds(q * width + r, local_rows, stride=BR), :] = (
                    total[r * local_rows:(r + 1) * local_rows]
                )
        load_rs[h + 1].wait()
        for s in range(local):
            forward(h + 1, s, rs_ref[h + 1, s] - nat[pl.ds(s * order, order), :])

    def hop(h, q, source, where, s_sem, r_sem, col):
        slot = above[h].at[
            pl.ds(((source * PAIR + col) * local + q) * row_blocks, row_blocks)
        ]
        return remote(slot, slot, s_sem, r_sem, where)

    def line_hop(h, q, k, source):
        return hop(h, q, source, peers[k], asend.at[h, q, k], arecv.at[h, q, k], x)

    def mate_hop(h, q, k, col):
        source = (z + line - k) % line
        return hop(h, q, source, mate, bsend.at[h, q, k], brecv.at[h, q, k], col)

    def publish(h, q):
        above[h][pl.ds((me * local + q) * row_blocks, row_blocks)] = (
            outs[h + 1][q].reshape(row_blocks, BR, cols).astype(jnp.bfloat16)
        )
        mate_hop(h, q, 0, x).start()
        for k in away:
            line_hop(h, q, k, z).start()

    for s in range(local):
        backward(levels - 1, s, low[levels - 1, s])
        publish(levels - 2, s)

    for h in range(levels - 2, -1, -1):
        if h > 0:
            prepare(h)
        for q in range(cut):
            for k in away:
                line_hop(h, q, k, (z + line - k) % line).wait_recv()
                mate_hop(h, q, k, x).start()
        for q in range(cut):
            for k in range(line):
                mate_hop(h, q, k, 1 - x).wait_recv()
        for s in range(local):
            for k in range(per_node):
                picked[pl.ds((s * per_node + k) * BR, BR), :] = above[h][
                    snode_s[h, s, k] * row_blocks + block_s[h, s, k]
                ]
            carried = low[h, s] - mm(
                od_t[h, s], picked[pl.ds(s * per_node * BR, per_node * BR), :]
            )
            backward(h, s, carried)
            if h > 0:
                publish(h - 1, s)

    for copy in sent:
        copy.wait_send()
    for h in range(levels - 1):
        for q in range(cut):
            for k in range(line):
                if h > 0 or (q, k) not in released:
                    x_copy(h, q, k).wait_send()
                mate_hop(h, q, k, x).wait_send()
            for k in away:
                z_copy(h, q, k).wait_send()
                line_hop(h, q, k, z).wait_send()


def dense_on_device(right_sides, diag_inverse, off_diagonal, target_snode, target_block):
    levels, local, order, cols = right_sides.shape
    n, parts = lax.axis_size("snode"), lax.axis_size("rhs")
    outgoing = local * target_snode.shape[2]
    row_blocks = order // BR
    local_rows = local * row_blocks
    line = n // PAIR
    ymany = parts // PAIR
    cut = local
    piece = (local_rows * BR // cut, cols)
    bf, f32 = jnp.bfloat16, jnp.float32
    steps = levels - 1
    dma = pltpu.SemaphoreType.DMA
    vmem = pl.BlockSpec(memory_space=pltpu.VMEM)
    smem = pl.BlockSpec(memory_space=pltpu.SMEM)
    hbm = pl.BlockSpec(memory_space=pltpu.HBM)
    answers = pl.pallas_call(
        functools.partial(dense_kernel, n, parts),
        out_shape=[[jax.ShapeDtypeStruct(right_sides.shape[1:], f32)] * levels],
        in_specs=[hbm] * 3 + [vmem] * 2 + [smem] * 2,
        out_specs=[[vmem] * levels],
        scratch_shapes=[
            pltpu.VMEM((levels, parts) + diag_inverse.shape[1:], f32),
            pltpu.VMEM((levels, local, 2, order, order), bf),
            pltpu.VMEM(off_diagonal.shape, bf),
            pltpu.VMEM((steps, local, order, off_diagonal.shape[2]), bf),
            pltpu.VMEM(right_sides.shape, f32),
            pltpu.VMEM(right_sides.shape, f32),
            pltpu.VMEM((outgoing * BR, cols), f32),
            pltpu.VMEM((local_rows * BR, cols), f32),
            pltpu.VMEM((steps, cut, n) + piece, bf),
            pltpu.VMEM((steps, cut, line) + piece, bf),
            pltpu.VMEM((steps, cut, line) + piece, bf),
            pltpu.VMEM((steps, cut, line) + piece, bf),
            [pltpu.VMEM((n * local_rows, BR, cols), bf)] * steps,
            pltpu.VMEM((outgoing * BR, cols), bf),
            dma((3, levels)),
            dma((levels, 2 * ymany)),
            dma((levels, 2 * ymany)),
            dma((steps, cut, line)),
            dma((steps, cut, line)),
            dma((steps, cut, line)),
            dma((steps, cut, line)),
            dma((steps, cut, line)),
            dma((steps, cut, line)),
            dma((steps, cut, line)),
            dma((steps, cut, line)),
            pltpu.SemaphoreType.REGULAR,
        ],
        compiler_params=pltpu.CompilerParams(
            collective_id=0, has_side_effects=True, vmem_limit_bytes=56 * 1024 * 1024
        ),
    )(right_sides, diag_inverse, off_diagonal, target_snode, target_block, target_snode,
      target_block)
    return jnp.stack(answers[0], axis=0)


def program(right_sides, diag_inverse, off_diagonal, target_snode, target_block):
    n, parts = lax.axis_size("snode"), lax.axis_size("rhs")
    capacity = 2 * right_sides.shape[1] * target_snode.shape[2] // n
    local_rows = right_sides.shape[1] * right_sides.shape[2] // BR
    dense = (
        capacity >= local_rows
        and n % PAIR == 0
        and parts % PAIR == 0
        and BR % right_sides.shape[1] == 0
    )
    body = dense_on_device if dense else on_device
    return body(right_sides, diag_inverse, off_diagonal, target_snode, target_block)


def solution(mesh):
    in_specs = (
        P(None, "snode", None, "rhs"),
        P(None, "snode", "rhs", None),
        P(None, "snode", None, None),
        P(None, "snode", None),
        P(None, "snode", None),
    )
    out_specs = P(None, "snode", None, "rhs")
    return jax.shard_map(
        program, mesh=mesh, in_specs=in_specs, out_specs=out_specs, check_vma=False
    )
```
